32 devices in a mesh: dp: 8 (over y, x, core), tensor: 4 (over z).
Axes of the slice: x: 2, y: 2, z: 4, core: 2. Of those that a mesh axis runs over, the one named last changes fastest.
Arguments:
- tokens_in: bfloat16 [12288, 1088], P(('dp', 'tensor')), may hold values from -6 to 6
- ln1_gain: bfloat16 [1088], replicated, may hold values from 0.5 to 1.5
- ln1_bias: bfloat16 [1088], replicated, may hold values from -3 to 3
- w_qkv: bfloat16 [3, 1088, 1088], P(None, 'tensor'), may hold values from -0.1875 to 0.1875
- b_qv: bfloat16 [2, 1088], replicated, may hold values from -4 to 4
- w_out: bfloat16 [1088, 1088], P('tensor'), may hold values from -0.75 to 0.75
- b_out: bfloat16 [1088], replicated, may hold values from -3 to 3
- ln2_gain: bfloat16 [1088], replicated, may hold values from 0.5 to 1.5
- ln2_bias: bfloat16 [1088], replicated, may hold values from -3 to 3
- w_up: bfloat16 [1088, 4352], P(None, 'tensor'), may hold values from -0.1875 to 0.1875
- b_up: bfloat16 [4352], P('tensor'), may hold values from -4 to 4
- w_down: bfloat16 [4352, 1088], P('tensor'), may hold values from -0.09375 to 0.09375
- b_down: bfloat16 [1088], replicated, may hold values from -3 to 3
- seq_lengths: int32 [6], replicated, may hold values from 1 to 4096, 12288 in all
- cotangent: bfloat16 [12288, 1088], P(('dp', 'tensor')), may hold values from -6 to 6
Outputs:
- block_out: bfloat16 [12288, 1088], P(('dp', 'tensor'))
- grad_input: float32 [12288, 1088], P(('dp', 'tensor'))
- grad_ln1_gain: float32 [1088], replicated
- grad_ln1_bias: float32 [1088], replicated
- grad_qkv: float32 [3, 1088, 1088], P(None, 'tensor', 'dp')
- grad_qv_bias: float32 [2, 1088], replicated
- grad_out: float32 [1088, 1088], P('tensor', 'dp')
- grad_out_bias: float32 [1088], replicated
- grad_ln2_gain: float32 [1088], replicated
- grad_ln2_bias: float32 [1088], replicated
- grad_up: float32 [1088, 4352], P('dp', 'tensor')
- grad_up_bias: float32 [4352], P('tensor')
- grad_down: float32 [4352, 1088], P('tensor', 'dp')
- grad_down_bias: float32 [1088], replicated
The draws below stay inside these ranges and needn't reach their ends.
Inputs may be any that keep to these rules, and one draw needn't show every extreme that they name: `seq_lengths`: the sequences lie one after another in token order; the lengths sum to 12288 and the longest is exactly 4096.
All inputs are finite; a program needn't handle non-finite values.
Results may differ from the reference program's by a relative error of at most 0.02.
Values may be sent and summed in bfloat16 or wider, within the bound.
No kernel may reach another device: no remote copies, remote signals or barrier semaphores. Data moves between devices by JAX's collectives and lax.ppermute only.
A program may use at most 192 MiB of HBM per device.

```python
import math
import jax
import jax.numpy as jnp
import numpy as np
from jax import lax

D = 1088
HEADS = 17
HEAD_DIM = 64
FF = 4352
TOK_DEV = 384
LONGEST = 4096
REACH = 11
TOKENS = 12288
SEQS = 6


def block_levels(key, extent, shards, least, top_value):
    def one(position, shards_of):
        draws = jax.random.uniform(jax.random.fold_in(jax.random.fold_in(key, 6), position), (shards_of,), jnp.float32, least / len(shards), top_value / len(shards))
        return jnp.repeat(jnp.exp(draws), extent[position] // shards_of).reshape((-1,) + (1,) * (len(extent) - position - 1))

    factor_of = one(*shards[0])
    for cut in shards[1:]:
        factor_of = factor_of * one(*cut)
    return factor_of


def profile(count, total, reach, lean):
    weights = [(1 << 20) // math.isqrt(rank ** lean) + 1 for rank in range(2, count + 1)]
    surplus, holding = total - reach - (count - 1), [1] * (count - 1)
    while surplus > 0:
        free = [i for i in range(count - 1) if holding[i] < reach]
        pool, budget = sum([weights[i] for i in free]), surplus
        for i in free:
            addition = min(reach - holding[i], max(1, budget * weights[i] // pool), surplus)
            holding[i] = holding[i] + addition
            surplus = surplus - addition
    return np.array([reach] + holding)


def uneven(rng, number_of, total, bound, skew):
    if number_of == 2:
        one = jax.random.randint(rng, (), max(1, total - bound), min(bound, total - 1) + 1)
        return jnp.stack([one, total - one])
    sizes = jnp.asarray(profile(number_of, total, bound, skew), jnp.int32)
    twos = (number_of - 1) // 2
    source_of, receiver = sizes[1:1 + 2 * twos:2], sizes[2:2 + 2 * twos:2]
    room = jnp.minimum(source_of - 1, bound - receiver)
    shifted = jax.random.randint(jax.random.fold_in(rng, 1), (twos,), 0, 1 << 20) % (room + 1)
    sizes = sizes.at[1:1 + 2 * twos:2].set(source_of - shifted).at[2:2 + 2 * twos:2].set(receiver + shifted)
    return sizes[jax.random.permutation(jax.random.fold_in(rng, 2), number_of)]


def gaussian(rng, dims, scale, bound, pieces=(), kind=jnp.bfloat16):
    entries = scale * jax.random.normal(rng, dims, jnp.float32)
    if pieces:
        entries = entries * block_levels(rng, dims, pieces, -0.22, 0.18)
    return jnp.clip(entries, -bound, bound).astype(kind)


def setup_inputs(seed: int = 0) -> dict:
    splits = jax.random.split(jax.random.key(seed), 16)
    return {
        "tokens_in": gaussian(splits[0], (TOKENS, D), 1.0, 6.0, ((0, 32),)),
        "ln1_gain": jnp.clip(1.0 + 0.1 * jax.random.normal(splits[1], (D,), jnp.float32), 0.5, 1.5).astype(jnp.bfloat16),
        "ln1_bias": gaussian(splits[2], (D,), 0.3, 3.0),
        "w_qkv": gaussian(splits[3], (3, D, D), D ** -0.5, 0.1875, ((1, 4),)),
        "b_qv": gaussian(splits[4], (2, D), 0.5, 4.0),
        "w_out": gaussian(splits[5], (D, D), 64 ** -0.5, 0.75, ((0, 4),)),
        "b_out": gaussian(splits[6], (D,), 0.3, 3.0),
        "ln2_gain": jnp.clip(1.0 + 0.1 * jax.random.normal(splits[7], (D,), jnp.float32), 0.5, 1.5).astype(jnp.bfloat16),
        "ln2_bias": gaussian(splits[8], (D,), 0.3, 3.0),
        "w_up": gaussian(splits[9], (D, FF), D ** -0.5, 0.1875, ((1, 4),)),
        "b_up": gaussian(splits[10], (FF,), 0.5, 4.0, ((0, 4),)),
        "w_down": gaussian(splits[11], (FF, D), FF ** -0.5, 0.09375, ((0, 4),)),
        "b_down": gaussian(splits[12], (D,), 0.3, 3.0),
        "seq_lengths": uneven(splits[13], SEQS, TOKENS, LONGEST, 2).astype(jnp.int32),
        "cotangent": gaussian(splits[14], (TOKENS, D), 1.0, 6.0, ((0, 32),)),
    }


norm_eps = 1e-05
score_scale = 0.125
masked_score = -1e+30

@jax.custom_vjp
def low(v):
    return lax.optimization_barrier(v.astype(jnp.bfloat16)).astype(jnp.float32)

@jax.custom_vjp
def low_back(v):
    return v

def low_keep(v):
    return (low(v), None)

def low_pass(kept, grad):
    return (grad,)

def back_keep(v):
    return (v, None)

def back_low(kept, grad):
    return (low(grad),)
low.defvjp(low_keep, low_pass)
low_back.defvjp(back_keep, back_low)

def layer_norm(values, gain_vec, bias_vec):
    mean_row = lax.optimization_barrier(jnp.mean(values, axis=-1, keepdims=True))
    centered = values - mean_row
    variance = lax.optimization_barrier(jnp.mean(centered * centered, axis=-1, keepdims=True))
    return centered * lax.rsqrt(variance + norm_eps) * gain_vec + bias_vec

def attend(queries, key_rows, value_rows, positions, segments):
    block_len = TOK_DEV
    span = (REACH + 1) * block_len
    lead = REACH * block_len
    key_pad = jnp.concatenate([jnp.zeros((lead, D), key_rows.dtype), key_rows], axis=0)
    value_pad = jnp.concatenate([jnp.zeros((lead, D), value_rows.dtype), value_rows], axis=0)
    pos_pad = jnp.concatenate([jnp.full((lead,), -1, jnp.int32), positions], axis=0)
    seg_pad = jnp.concatenate([jnp.full((lead,), -1, jnp.int32), segments], axis=0)

    def one_block(counter):
        start = (counter * block_len).astype(jnp.int32)
        query_heads = lax.dynamic_slice_in_dim(queries, start, block_len, 0).reshape(block_len, HEADS, HEAD_DIM)
        key_heads = lax.dynamic_slice_in_dim(key_pad, start, span, 0).reshape(span, HEADS, HEAD_DIM)
        value_heads = lax.dynamic_slice_in_dim(value_pad, start, span, 0).reshape(span, HEADS, HEAD_DIM)
        query_pos = lax.dynamic_slice_in_dim(positions, start, block_len, 0)
        query_seg = lax.dynamic_slice_in_dim(segments, start, block_len, 0)
        key_pos = lax.dynamic_slice_in_dim(pos_pad, start, span, 0)
        key_seg = lax.dynamic_slice_in_dim(seg_pad, start, span, 0)
        allowed = (query_seg[:, None] == key_seg[None, :]) & (key_pos[None, :] <= query_pos[:, None]) & (key_pos[None, :] >= 0)
        scores = low_back(jnp.einsum('qhd,khd->hqk', query_heads, key_heads, precision=lax.Precision.HIGHEST) * score_scale)
        masked = jnp.where(allowed[None], scores, masked_score)
        running_max = lax.optimization_barrier(jnp.max(masked, axis=2, keepdims=True))
        weights = jnp.where(allowed[None], jnp.exp(masked - running_max), 0.0)
        probs = low(weights / lax.optimization_barrier(jnp.sum(weights, axis=2, keepdims=True)))
        mixed_heads = jnp.einsum('hqk,khd->qhd', probs, value_heads, precision=lax.Precision.HIGHEST)
        return mixed_heads.reshape(block_len, D)
    blocks = lax.map(jax.checkpoint(one_block), jnp.arange(TOKENS // block_len, dtype=jnp.int32))
    return blocks.reshape(TOKENS, D)

def block_forward(stream, gain_one, shift_one, w_qkv, b_qv, w_out, b_out, gain_two, shift_two, w_up, b_up, w_down, b_down, positions, segments):
    highest = lax.Precision.HIGHEST
    normed_one = low(layer_norm(stream, gain_one, shift_one))
    queries = low_back(low(jnp.dot(normed_one, w_qkv[0].T, precision=highest) + b_qv[0]))
    key_rows = low_back(low(jnp.dot(normed_one, w_qkv[1].T, precision=highest)))
    value_rows = low_back(low(jnp.dot(normed_one, w_qkv[2].T, precision=highest) + b_qv[1]))
    attended = low_back(low(attend(queries, key_rows, value_rows, positions, segments)))
    stream_one = stream + low_back(jnp.dot(attended, w_out, precision=highest) + b_out)
    normed_two = low(layer_norm(stream_one, gain_two, shift_two))
    hidden_pre = low_back(jnp.dot(normed_two, w_up, precision=highest) + b_up)
    activated = low(jax.nn.gelu(hidden_pre, approximate=True))
    branch_two = low_back(jnp.dot(activated, w_down, precision=highest) + b_down)
    return stream_one + branch_two

def reference(tokens_in, ln1_gain, ln1_bias, w_qkv, b_qv, w_out, b_out, ln2_gain, ln2_bias, w_up, b_up, w_down, b_down, seq_lengths, cotangent):
    seq_ends = jnp.cumsum(seq_lengths).astype(jnp.int32)
    positions = jnp.arange(TOKENS, dtype=jnp.int32)
    segments = lax.optimization_barrier(jnp.sum((positions[:, None] >= seq_ends[None, :]).astype(jnp.int32), axis=1)).astype(jnp.int32)
    floats = [argument.astype(jnp.float32) for argument in (tokens_in, ln1_gain, ln1_bias, w_qkv, b_qv, w_out, b_out, ln2_gain, ln2_bias, w_up, b_up, w_down, b_down)]

    def forward(*params):
        return block_forward(*params, positions, segments)
    result, pull = jax.vjp(forward, *floats)
    grads = pull(cotangent.astype(jnp.float32))
    return (result.astype(jnp.bfloat16), grads[0], grads[1], grads[2], grads[3], grads[4], grads[5], grads[6], grads[7], grads[8], grads[9], grads[10], grads[11], grads[12])
```

```python
import functools

import jax
import jax.numpy as jnp
from jax import lax
from jax.experimental import pallas as pl
from jax.experimental.pallas import tpu as pltpu
from jax.sharding import PartitionSpec as P

HEADS = 17
HEAD_DIM = 64
REACH = 11

norm_eps = 1e-05
score_scale = 0.125
masked_score = -1e30
everywhere = ("dp", "tensor")


def line(count, steps):
    first, last = (max(0, -steps), min(count, count - steps))
    return [(source, source + steps) for source in range(first, last)]


def gather_tensor(rows, axis):
    count = lax.axis_size("tensor")
    index = lax.axis_index("tensor")
    up, down = [rows], [rows]
    for _ in range(count - 1):
        up.append(lax.ppermute(up[-1], "tensor", line(count, 1)))
        down.append(lax.ppermute(down[-1], "tensor", line(count, -1)))
    shape = rows.shape[:axis] + (count,) + rows.shape[axis:]
    gathered = lax.dynamic_update_index_in_dim(jnp.zeros(shape, rows.dtype), rows, index, axis)
    for steps in range(1, count):
        block = jnp.where(index >= steps, up[steps], down[count - steps])
        gathered = lax.dynamic_update_index_in_dim(
            gathered, block, lax.rem(index - steps + count, count), axis
        )
    return gathered


def scatter_tensor(partial_sum):
    arrived = lax.all_to_all(
        partial_sum.astype(jnp.bfloat16), "tensor", split_axis=0, concat_axis=0, tiled=True
    )
    return jnp.sum(arrived.astype(jnp.float32), axis=0)


def scatter_dp(partial_sum, axis):
    return lax.psum_scatter(
        partial_sum.astype(jnp.bfloat16), "dp", scatter_dimension=axis, tiled=True
    ).astype(jnp.float32)


def norm_forward(values, gain_vec, bias_vec):
    mean_row = jnp.mean(values, axis=1, keepdims=True)
    centered = values - mean_row
    variance = jnp.mean(centered * centered, axis=1, keepdims=True)
    inv_std = lax.rsqrt(variance + norm_eps)
    normed = centered * inv_std
    return (normed, inv_std, normed * gain_vec + bias_vec)


def norm_backward(grad_normed, normed, inv_std, gain_vec):
    scaled = grad_normed * gain_vec
    plain_mean = jnp.mean(scaled, axis=1, keepdims=True)
    cross_mean = jnp.mean(scaled * normed, axis=1, keepdims=True)
    grad_values = inv_std * (scaled - plain_mean - normed * cross_mean)
    return (grad_values, jnp.sum(grad_normed * normed, axis=0), jnp.sum(grad_normed, axis=0))


def tile_of(width):
    return 384 if width % 384 == 0 else width


def attention_plan(query_pos, key_base, key_offsets, seq_ends):
    width = query_pos.shape[1]
    key_width = key_offsets.shape[0]
    tile, key_tile = tile_of(width), tile_of(key_width)
    starts = jnp.max(
        jnp.where(seq_ends[None, None, :] <= query_pos[:, :, None], seq_ends[None, None, :], 0),
        axis=2,
    )
    rows = jnp.stack((query_pos, starts), axis=1)
    tiles = query_pos.reshape(-1, tile)
    first, last = tiles[:, 0], tiles[:, tile - 1]
    last_start = starts.reshape(-1, tile)[:, tile - 1]
    offset_tiles = key_offsets.reshape(-1, key_tile)
    key_min = (key_base[:, None] + offset_tiles[None, :, 0]).reshape(-1)
    key_max = (key_base[:, None] + offset_tiles[None, :, key_tile - 1]).reshape(-1)
    key_end = jnp.min(
        jnp.where(seq_ends[None, :] > key_max[:, None], seq_ends[None, :], seq_ends[-1]), axis=1
    )
    low = jnp.sum((last[None, :] < key_min[:, None]).astype(jnp.int32), axis=1)
    high = jnp.sum((first[None, :] < key_end[:, None]).astype(jnp.int32), axis=1)
    bases = jnp.repeat(key_base, key_width // key_tile)
    plan = jnp.concatenate((low, high, bases, key_min, key_max, first, last_start))
    return (plan.astype(jnp.int32), rows.astype(jnp.int32), key_offsets[:, None].astype(jnp.int32))


def key_allowed(column_ref, rows_ref, step, per_key, key_tile, base, group, lanes):
    offset = pl.multiple_of(lax.rem(step, per_key) * key_tile, key_tile)
    key_pos = column_ref[pl.ds(offset, key_tile), :] + base
    query_pos = rows_ref[group, 0:1, lanes]
    query_start = rows_ref[group, 1:2, lanes]
    return (key_pos <= query_pos) & (key_pos >= query_start)


def forward_kernel(
    dims, plan_ref, query_ref, pair_ref, rows_ref, column_ref, out_ref, total_ref, acc, top, tot
):
    blocks, groups, per_query, per_key, tile, key_tile = dims
    count = groups * per_query
    step = pl.program_id(0)

    @pl.when(step == 0)
    def _():
        acc[...] = jnp.zeros_like(acc)
        tot[...] = jnp.zeros_like(tot)
        top[...] = jnp.full(top.shape, masked_score, jnp.float32)

    keys = jnp.transpose(pair_ref[0, :HEAD_DIM, :].astype(jnp.float32)).astype(jnp.bfloat16)
    values_t = pair_ref[0, HEAD_DIM:, :]
    base, key_min, key_max = (plan_ref[kind * blocks + step] for kind in (2, 3, 4))

    def one_tile(index, _):
        group = lax.div(index, per_query)
        lanes = pl.ds(pl.multiple_of(lax.rem(index, per_query) * tile, tile), tile)
        queries_t = query_ref[group, :HEAD_DIM, lanes] * jnp.bfloat16(score_scale)
        inside = (key_max <= plan_ref[5 * blocks + index]) & (
            key_min >= plan_ref[5 * blocks + count + index]
        )

        def update(masked):
            scores = jnp.dot(keys, queries_t, preferred_element_type=jnp.float32)
            if masked:
                allowed = key_allowed(
                    column_ref, rows_ref, step, per_key, key_tile, base, group, lanes
                )
                scores = jnp.where(allowed, scores, masked_score)
            old_top = top[index]
            new_top = jnp.maximum(old_top, jnp.max(scores, axis=0, keepdims=True))
            weights = jnp.exp(scores - new_top)
            shrink = jnp.exp(old_top - new_top)
            top[index] = new_top
            tot[index] = tot[index] * shrink + jnp.sum(weights, axis=0, keepdims=True)
            acc[index] = acc[index] * shrink + jnp.dot(
                values_t, weights.astype(jnp.bfloat16), preferred_element_type=jnp.float32
            )

        pl.when(inside)(lambda: update(False))
        pl.when(jnp.logical_not(inside))(lambda: update(True))
        return 0

    lax.fori_loop(plan_ref[step], plan_ref[blocks + step], one_tile, 0)

    @pl.when(step == blocks - 1)
    def _():
        def finish(index, _):
            group = lax.div(index, per_query)
            lanes = pl.ds(pl.multiple_of(lax.rem(index, per_query) * tile, tile), tile)
            out_ref[group, :, lanes] = acc[index] / tot[index]
            total_ref[index] = top[index] + jnp.log(tot[index])
            return 0

        lax.fori_loop(0, count, finish, 0)


def backward_kernel(
    dims,
    plan_ref,
    query_ref,
    pair_ref,
    rows_ref,
    column_ref,
    grad_ref,
    out_ref,
    total_ref,
    query_grad_ref,
    pair_grad_ref,
    acc,
    inner,
    query_rows,
    grad_rows,
    key_acc,
    value_acc,
):
    blocks, groups, per_query, per_key, tile, key_tile = dims
    count = groups * per_query
    step = pl.program_id(0)

    @pl.when(step == 0)
    def _():
        acc[...] = jnp.zeros_like(acc)

        def prepare(index, _):
            group = lax.div(index, per_query)
            lanes = pl.ds(pl.multiple_of(lax.rem(index, per_query) * tile, tile), tile)
            grads = grad_ref[group, :, lanes].astype(jnp.float32)
            inner[index] = jnp.sum(grads * out_ref[group, :, lanes], axis=0, keepdims=True)
            grad_rows[index] = jnp.transpose(grads).astype(jnp.bfloat16)
            scaled = query_ref[group, :HEAD_DIM, lanes].astype(jnp.float32) * score_scale
            query_rows[index] = jnp.transpose(scaled).astype(jnp.bfloat16)
            return 0

        lax.fori_loop(0, count, prepare, 0)

    keys_t = pair_ref[0, :HEAD_DIM, :]
    keys = jnp.transpose(keys_t.astype(jnp.float32)).astype(jnp.bfloat16)
    values = jnp.transpose(pair_ref[0, HEAD_DIM:, :].astype(jnp.float32)).astype(jnp.bfloat16)
    base, key_min, key_max = (plan_ref[kind * blocks + step] for kind in (2, 3, 4))
    key_acc[...] = jnp.zeros_like(key_acc)
    value_acc[...] = jnp.zeros_like(value_acc)

    def one_tile(index, _):
        group = lax.div(index, per_query)
        lanes = pl.ds(pl.multiple_of(lax.rem(index, per_query) * tile, tile), tile)
        queries_t = query_ref[group, :HEAD_DIM, lanes] * jnp.bfloat16(score_scale)
        grads_t = grad_ref[group, :, lanes]
        inside = (key_max <= plan_ref[5 * blocks + index]) & (
            key_min >= plan_ref[5 * blocks + count + index]
        )

        def update(masked):
            scores = jnp.dot(keys, queries_t, preferred_element_type=jnp.float32)
            weights = jnp.exp(scores - total_ref[index])
            if masked:
                allowed = key_allowed(
                    column_ref, rows_ref, step, per_key, key_tile, base, group, lanes
                )
                weights = jnp.where(allowed, weights, 0.0)
            grad_weights = jnp.dot(values, grads_t, preferred_element_type=jnp.float32)
            grad_scores = (weights * (grad_weights - inner[index])).astype(jnp.bfloat16)
            value_acc[...] += jnp.dot(
                weights.astype(jnp.bfloat16), grad_rows[index], preferred_element_type=jnp.float32
            )
            key_acc[...] += jnp.dot(
                grad_scores, query_rows[index], preferred_element_type=jnp.float32
            )
            acc[index] += jnp.dot(keys_t, grad_scores, preferred_element_type=jnp.float32)

        pl.when(inside)(lambda: update(False))
        pl.when(jnp.logical_not(inside))(lambda: update(True))
        return 0

    lax.fori_loop(plan_ref[step], plan_ref[blocks + step], one_tile, 0)
    pair_grad_ref[0, :HEAD_DIM, :] = jnp.transpose(key_acc[...]).astype(jnp.bfloat16)
    pair_grad_ref[0, HEAD_DIM:, :] = jnp.transpose(value_acc[...]).astype(jnp.bfloat16)

    @pl.when(step == blocks - 1)
    def _():
        def finish(index, _):
            group = lax.div(index, per_query)
            lanes = pl.ds(pl.multiple_of(lax.rem(index, per_query) * tile, tile), tile)
            query_grad_ref[group, :, lanes] = (acc[index] * score_scale).astype(jnp.bfloat16)
            return 0

        lax.fori_loop(0, count, finish, 0)


def attention_call(kernel, queries, pairs, plan, more, outs, scratch, flops):
    numbers, rows, column = plan
    groups, _, width = queries.shape
    key_groups, _, key_width = pairs.shape
    tile, key_tile = tile_of(width), tile_of(key_width)
    per_query, per_key = width // tile, key_width // key_tile
    blocks = key_groups * per_key
    count = groups * per_query

    def whole(array):
        return pl.BlockSpec(array.shape, lambda step, plan_ref: (0,) * array.ndim)

    pair_spec = pl.BlockSpec(
        (1, 2 * HEAD_DIM, key_tile),
        lambda step, plan_ref: (lax.div(step, per_key), 0, lax.rem(step, per_key)),
    )
    out_shapes, out_specs = [], []
    for kind in outs:
        if kind == "pairs":
            out_shapes.append(jax.ShapeDtypeStruct(pairs.shape, jnp.bfloat16))
            out_specs.append(pair_spec)
        else:
            shape = (count, 1, tile) if kind == "total" else (groups, HEAD_DIM, width)
            dtype = jnp.bfloat16 if kind == "grads" else jnp.float32
            out_shapes.append(jax.ShapeDtypeStruct(shape, dtype))
            out_specs.append(whole(out_shapes[-1]))
    sizes = {
        "acc": pltpu.VMEM((count, HEAD_DIM, tile), jnp.float32),
        "row": pltpu.VMEM((count, 1, tile), jnp.float32),
        "rows": pltpu.VMEM((count, tile, HEAD_DIM), jnp.bfloat16),
        "keys": pltpu.VMEM((key_tile, HEAD_DIM), jnp.float32),
    }
    pairs_near = groups * width * min(key_groups * key_width, 2304)
    return pl.pallas_call(
        functools.partial(kernel, (blocks, groups, per_query, per_key, tile, key_tile)),
        out_shape=out_shapes,
        grid_spec=pltpu.PrefetchScalarGridSpec(
            num_scalar_prefetch=1,
            grid=(blocks,),
            in_specs=[whole(queries), pair_spec, whole(rows), whole(column)]
            + [whole(array) for array in more],
            out_specs=out_specs,
            scratch_shapes=[sizes[name] for name in scratch],
        ),
        compiler_params=pltpu.CompilerParams(
            dimension_semantics=("arbitrary",), vmem_limit_bytes=56 * 2**20
        ),
        cost_estimate=pl.CostEstimate(
            flops=flops * pairs_near * HEAD_DIM,
            bytes_accessed=4 * queries.size + 4 * pairs.size,
            transcendentals=pairs_near,
        ),
    )(numbers, queries, pairs, rows, column, *more)


def attend(queries, pairs, plan):
    return attention_call(
        forward_kernel, queries, pairs, plan, (), ("out", "total"), ("acc", "row", "row"), 16
    )


def attend_back(queries, pairs, plan, grads, out, total):
    return attention_call(
        backward_kernel,
        queries,
        pairs,
        plan,
        (grads, out, total),
        ("grads", "pairs"),
        ("acc", "row", "rows", "rows", "keys", "keys"),
        40,
    )


def aligned_weights(stacked, tensor_size, tensor_index, head_rows):
    slab = stacked.shape[1]
    extra = slab - head_rows
    most = (tensor_size - 1) * extra
    before = lax.ppermute(stacked[:, slab - most :], "tensor", line(tensor_size, 1))
    joined = jnp.concatenate((before, stacked), axis=1)
    own = lax.dynamic_slice_in_dim(joined, most - extra * tensor_index, head_rows, 1)
    final = stacked[:, slab - HEAD_DIM :]
    last = jnp.where(tensor_index == tensor_size - 1, final, jnp.zeros_like(final))
    for target in range(tensor_size - 1):
        last = last + lax.ppermute(final, "tensor", [(tensor_size - 1, target)])
    return own, last


def slab_rows(own, last, slab, tensor_size, tensor_index):
    extra = slab - own.shape[1]
    most = (tensor_size - 1) * extra
    after = lax.ppermute(own[:, :most], "tensor", line(tensor_size, -1))
    after = jnp.pad(after, ((0, 0), (0, HEAD_DIM - most), (0, 0)))
    after = jnp.where(tensor_index == tensor_size - 1, last, after)
    joined = jnp.concatenate((own, after), axis=1)
    return lax.dynamic_slice_in_dim(joined, extra * tensor_index, slab, 1)


def local(
    tokens_in,
    ln1_gain,
    ln1_bias,
    w_qkv,
    b_qv,
    w_out,
    b_out,
    ln2_gain,
    ln2_bias,
    w_up,
    b_up,
    w_down,
    b_down,
    seq_lengths,
    cotangent,
):
    tensor_size = lax.axis_size("tensor")
    tensor_index = lax.axis_index("tensor")
    dp_size = lax.axis_size("dp")
    dp_index = lax.axis_index("dp")
    flat_index = dp_index * tensor_size + tensor_index
    rows, width = tokens_in.shape
    slab = w_qkv.shape[1]
    unit_slab = w_up.shape[1]
    slots = (HEADS - 1) // tensor_size
    members = dp_size // slots
    member = lax.rem(dp_index, members)
    part = rows // members
    lanes = tensor_size * part
    head_rows = slots * HEAD_DIM
    low = jnp.bfloat16
    seq_ends = jnp.cumsum(seq_lengths)
    gain_one = ln1_gain.astype(jnp.float32)
    shift_one = ln1_bias.astype(jnp.float32)
    gain_two = ln2_gain.astype(jnp.float32)
    shift_two = ln2_bias.astype(jnp.float32)

    stream = tokens_in.astype(jnp.float32)
    normed_one, inv_one, pre_one = norm_forward(stream, gain_one, shift_one)
    pre_one = pre_one.astype(low)
    wide_one = gather_tensor(pre_one.reshape(members, part, width), 1)
    wide_one = wide_one.reshape(members, lanes, width)
    stacked = jnp.concatenate((w_qkv, w_out[None]), axis=0)
    own_w, last_w = aligned_weights(stacked, tensor_size, tensor_index, head_rows)
    head_w = own_w.reshape(4, slots, HEAD_DIM, width).transpose(1, 0, 2, 3)
    qkv_w = head_w[:, :3].reshape(slots, 3 * HEAD_DIM, width)
    out_w = head_w[:, 3]
    last_qkv_w = last_w[:3].reshape(3 * HEAD_DIM, width)
    last_out_w = last_w[3]
    bias_full = jnp.stack((b_qv[0], jnp.zeros_like(b_qv[0]), b_qv[1])).astype(jnp.float32)
    own_bias = lax.dynamic_slice_in_dim(bias_full, tensor_index * head_rows, head_rows, 1)
    own_bias = own_bias.reshape(3, slots, HEAD_DIM).transpose(1, 0, 2).reshape(slots, -1)
    last_bias = bias_full[:, width - HEAD_DIM :].reshape(-1)

    offsets = jnp.arange(tensor_size, dtype=jnp.int32)[:, None] * rows
    offsets = (offsets + jnp.arange(part, dtype=jnp.int32)[None]).reshape(-1)
    dp_starts = jnp.arange(dp_size, dtype=jnp.int32) * (tensor_size * rows)
    query_pos = dp_starts[:, None] + offsets[None] + member * part
    halves = jnp.arange(members, dtype=jnp.int32)
    if members == 2:
        halves = lax.rem(member + halves, 2)
    key_base = (halves[:, None] * part + dp_starts[None]).reshape(-1)
    plan = attention_plan(query_pos, key_base, offsets, seq_ends)
    row_range = jnp.arange(rows, dtype=jnp.int32)
    reach = min(REACH + 1, dp_size * tensor_size)
    window = jnp.clip(flat_index - REACH, 0, dp_size * tensor_size - reach)
    last_base = (window + jnp.arange(reach, dtype=jnp.int32)) * rows
    last_plan = attention_plan(
        (flat_index * rows + row_range)[None], last_base, row_range, seq_ends
    )

    qkv = jnp.einsum("cfd,gtd->cgft", qkv_w, wide_one, preferred_element_type=jnp.float32)
    qkv = (qkv + own_bias[:, None, :, None]).astype(low).reshape(dp_size, 3 * HEAD_DIM, lanes)
    qkv = lax.all_to_all(qkv, "dp", split_axis=0, concat_axis=0, tiled=True)
    last_qkv = jnp.einsum("fd,td->ft", last_qkv_w, pre_one, preferred_element_type=jnp.float32)
    last_qkv = (last_qkv + last_bias[:, None]).astype(low)[None]
    last_pairs = lax.all_gather(last_qkv[:, HEAD_DIM:], everywhere, axis=0, tiled=True)
    last_pairs = lax.dynamic_slice_in_dim(last_pairs, window, reach, 0)

    swap = [(i, i ^ 1) for i in range(dp_size)]
    sharing = [list(range(i, i + members)) for i in range(0, dp_size, members)]
    own_pairs = qkv[:, HEAD_DIM:]
    if members == 2:
        pairs = jnp.concatenate((own_pairs, lax.ppermute(own_pairs, "dp", swap)), axis=0)
    else:
        pairs = lax.all_gather(own_pairs, "dp", axis_index_groups=sharing, axis=0, tiled=True)
    mixed, total = attend(qkv, pairs, plan)
    last_mixed, last_total = attend(last_qkv, last_pairs, last_plan)
    attended = lax.all_to_all(mixed.astype(low), "dp", split_axis=0, concat_axis=0, tiled=True)
    attended = attended.reshape(slots, members, HEAD_DIM, lanes)
    last_attended = last_mixed[0].astype(low)

    contract_first = (((0,), (0,)), ((), ()))
    contract_cols = (((1,), (1,)), ((), ()))
    branch = jnp.einsum("cgft,cfd->gtd", attended, out_w, preferred_element_type=jnp.float32)
    branch = branch.astype(low).reshape(members, tensor_size, part, width).transpose(1, 0, 2, 3)
    branch = scatter_tensor(branch.reshape(tensor_size, rows, width))
    last_branch = lax.dot_general(
        last_attended, last_out_w, contract_first, preferred_element_type=jnp.float32
    )
    stream_one = stream + (branch + last_branch) + b_out.astype(jnp.float32)
    normed_two, inv_two, pre_two = norm_forward(stream_one, gain_two, shift_two)
    wide_two = gather_tensor(pre_two.astype(low), 0).reshape(tensor_size * rows, width)
    hidden_pre = jnp.dot(wide_two, w_up, preferred_element_type=jnp.float32) + b_up.astype(
        jnp.float32
    )
    gelu_out, gelu_pull = jax.vjp(
        lambda hidden_in: jax.nn.gelu(hidden_in, approximate=True), hidden_pre
    )
    activated = gelu_out.astype(low)
    down_sum = jnp.dot(activated, w_down, preferred_element_type=jnp.float32)
    down_sum = scatter_tensor(down_sum.reshape(tensor_size, rows, width))
    block_out = (stream_one + down_sum + b_down.astype(jnp.float32)).astype(low)

    grad_two = cotangent.astype(jnp.float32)
    grad_down_bias = jnp.sum(grad_two, axis=0)
    wide_grad = gather_tensor(cotangent, 0).reshape(tensor_size * rows, width)
    grad_act = lax.dot_general(wide_grad, w_down, contract_cols, preferred_element_type=jnp.float32)
    grad_down = lax.dot_general(
        activated, wide_grad, contract_first, preferred_element_type=jnp.float32
    )
    grad_hidden = gelu_pull(grad_act)[0].astype(low)
    grad_up_part = jnp.sum(grad_hidden.astype(jnp.float32), axis=0)
    grad_up = lax.dot_general(
        wide_two, grad_hidden, contract_first, preferred_element_type=jnp.float32
    )
    grad_normed_two = lax.dot_general(
        grad_hidden, w_up, contract_cols, preferred_element_type=jnp.float32
    )
    grad_normed_two = scatter_tensor(grad_normed_two.reshape(tensor_size, rows, width))
    grad_res_two, grad_gain_two, grad_shift_two = norm_backward(
        grad_normed_two, normed_two, inv_two, gain_two
    )
    grad_stream_one = grad_two + grad_res_two
    grad_branch = grad_stream_one.astype(low)
    grad_out_bias = jnp.sum(grad_branch.astype(jnp.float32), axis=0)
    wide_branch = gather_tensor(grad_branch.reshape(members, part, width), 1)
    wide_branch = wide_branch.reshape(members, lanes, width)
    last_grads = lax.dot_general(
        last_out_w, grad_branch, contract_cols, preferred_element_type=jnp.float32
    )
    last_grads = last_grads.astype(low)[None]
    grads = jnp.einsum("cfd,gtd->cgft", out_w, wide_branch, preferred_element_type=jnp.float32)
    grads = grads.astype(low).reshape(dp_size, HEAD_DIM, lanes)
    grads = lax.all_to_all(grads, "dp", split_axis=0, concat_axis=0, tiled=True)
    last_query_grad, last_pair_grad = attend_back(
        last_qkv, last_pairs, last_plan, last_grads, last_mixed, last_total
    )
    last_pair_grad = lax.dynamic_update_slice_in_dim(
        jnp.zeros((dp_size * tensor_size, 2 * HEAD_DIM, rows), low), last_pair_grad, window, 0
    )
    last_pair_grad = lax.psum_scatter(last_pair_grad, everywhere, scatter_dimension=0, tiled=True)
    query_grad, pair_grad = attend_back(qkv, pairs, plan, grads, mixed, total)
    pair_grad = pair_grad.reshape(members, dp_size, 2 * HEAD_DIM, lanes)
    if members == 2:
        other_grad = lax.ppermute(pair_grad[1], "dp", swap)
        pair_sum = pair_grad[0].astype(jnp.float32) + other_grad.astype(jnp.float32)
    else:
        pair_grad = lax.all_to_all(
            pair_grad, "dp", 0, 0, axis_index_groups=sharing, tiled=True
        )
        pair_sum = jnp.sum(pair_grad.astype(jnp.float32), axis=0)
    qkv_grad = jnp.concatenate((query_grad, pair_sum.astype(low)), axis=1)
    qkv_grad = lax.all_to_all(qkv_grad, "dp", split_axis=0, concat_axis=0, tiled=True)
    qkv_grad = qkv_grad.reshape(slots, members, 3 * HEAD_DIM, lanes)
    last_qkv_grad = jnp.concatenate((last_query_grad[0], last_pair_grad[0]), axis=0)

    grad_normed_one = jnp.einsum(
        "cgft,cfd->gtd", qkv_grad, qkv_w, preferred_element_type=jnp.float32
    )
    grad_normed_one = grad_normed_one.astype(low).reshape(members, tensor_size, part, width)
    grad_normed_one = scatter_tensor(
        grad_normed_one.transpose(1, 0, 2, 3).reshape(tensor_size, rows, width)
    )
    last_normed_one = lax.dot_general(
        last_qkv_grad, last_qkv_w, contract_first, preferred_element_type=jnp.float32
    )
    grad_normed_one = grad_normed_one + last_normed_one
    grad_res_one, grad_gain_one, grad_shift_one = norm_backward(
        grad_normed_one, normed_one, inv_one, gain_one
    )
    grad_input = grad_stream_one + grad_res_one

    own_qkv_grad = jnp.einsum(
        "cgft,gtd->cfd", qkv_grad, wide_one, preferred_element_type=jnp.float32
    )
    own_qkv_grad = own_qkv_grad.reshape(slots, 3, HEAD_DIM, width).transpose(1, 0, 2, 3)
    own_qkv_grad = own_qkv_grad.reshape(3, head_rows, width).astype(low)
    own_out_grad = jnp.einsum(
        "cgft,gtd->cfd", attended, wide_branch, preferred_element_type=jnp.float32
    )
    own_out_grad = own_out_grad.reshape(1, head_rows, width).astype(low)
    last_qkv_part = jnp.dot(last_qkv_grad, pre_one, preferred_element_type=jnp.float32)
    last_out_part = jnp.dot(last_attended, grad_branch, preferred_element_type=jnp.float32)
    last_parts = jnp.concatenate((last_qkv_part, last_out_part), axis=0).astype(low)
    last_parts = lax.psum(last_parts, "tensor").reshape(4, HEAD_DIM, width)
    grad_qkv = slab_rows(own_qkv_grad, last_parts[:3], slab, tensor_size, tensor_index)
    grad_out = slab_rows(own_out_grad, last_parts[3:], slab, tensor_size, tensor_index)[0]

    qkv_sums = jnp.sum(qkv_grad.astype(jnp.float32), axis=(1, 3)).reshape(slots, 3, HEAD_DIM)
    qkv_sums = qkv_sums.transpose(1, 0, 2).reshape(3, head_rows)
    last_sums = jnp.sum(last_qkv_grad.astype(jnp.float32), axis=1).reshape(3, HEAD_DIM)
    sums_full = jnp.zeros((3, width), jnp.float32).at[:, width - HEAD_DIM :].set(last_sums)
    sums_full = lax.dynamic_update_slice_in_dim(
        sums_full, qkv_sums, tensor_index * head_rows, 1
    )
    grad_qv_bias = jnp.stack((sums_full[0], sums_full[2]))
    up_full = lax.dynamic_update_slice_in_dim(
        jnp.zeros((unit_slab * tensor_size,), jnp.float32),
        grad_up_part,
        tensor_index * unit_slab,
        0,
    )
    early = lax.psum(
        (grad_out_bias, grad_gain_two, grad_shift_two, up_full, grad_down_bias), everywhere
    )
    late = lax.psum((grad_gain_one, grad_shift_one, grad_qv_bias), everywhere)
    grad_up_bias = lax.dynamic_slice_in_dim(early[3], tensor_index * unit_slab, unit_slab, 0)
    return (
        block_out,
        grad_input,
        late[0],
        late[1],
        scatter_dp(grad_qkv, 2),
        late[2],
        scatter_dp(grad_out, 1),
        early[0],
        early[1],
        early[2],
        scatter_dp(grad_up, 0),
        grad_up_bias,
        scatter_dp(grad_down, 1),
        early[4],
    )


def solution(mesh):
    in_specs = (
        P(("dp", "tensor"), None),
        P(),
        P(),
        P(None, "tensor", None),
        P(),
        P("tensor", None),
        P(),
        P(),
        P(),
        P(None, "tensor"),
        P("tensor"),
        P("tensor", None),
        P(),
        P(),
        P(("dp", "tensor"), None),
    )
    out_specs = (
        P(("dp", "tensor"), None),
        P(("dp", "tensor"), None),
        P(),
        P(),
        P(None, "tensor", "dp"),
        P(),
        P("tensor", "dp"),
        P(),
        P(),
        P(),
        P("dp", "tensor"),
        P("tensor"),
        P("tensor", "dp"),
        P(),
    )
    return jax.shard_map(local, mesh=mesh, in_specs=in_specs, out_specs=out_specs, check_vma=False)
```

```python
import functools

import jax
import jax.numpy as jnp
from jax import lax
from jax.experimental import pallas as pl
from jax.experimental.pallas import tpu as pltpu
from jax.sharding import PartitionSpec as P

HEADS = 17
HEAD_DIM = 64
REACH = 11

norm_eps = 1e-05
score_scale = 0.125
masked_score = -1e30
everywhere = ("chip", "core", "tensor")
layer = ("chip", "core")
sharers = ("tensor", "chip")


def line(count, steps):
    first, last = (max(0, -steps), min(count, count - steps))
    return [(source, source + steps) for source in range(first, last)]


def gather_tensor(rows, axis):
    count = lax.axis_size("tensor")
    index = lax.axis_index("tensor")
    up, down = [rows], [rows]
    for _ in range(count - 1):
        up.append(lax.ppermute(up[-1], "tensor", line(count, 1)))
        down.append(lax.ppermute(down[-1], "tensor", line(count, -1)))
    shape = rows.shape[:axis] + (count,) + rows.shape[axis:]
    gathered = lax.dynamic_update_index_in_dim(jnp.zeros(shape, rows.dtype), rows, index, axis)
    for steps in range(1, count):
        block = jnp.where(index >= steps, up[steps], down[count - steps])
        gathered = lax.dynamic_update_index_in_dim(
            gathered, block, lax.rem(index - steps + count, count), axis
        )
    return gathered


def scatter_tensor(partial_sum):
    arrived = lax.all_to_all(partial_sum, "tensor", split_axis=0, concat_axis=0, tiled=True)
    return jnp.sum(arrived.astype(jnp.float32), axis=0)


def after(value, token):
    return lax.optimization_barrier((value, token))[0]


def other_core(value):
    return lax.ppermute(value, "core", [(0, 1), (1, 0)])


def small_sum(value):
    count = lax.axis_size(everywhere)
    copies = jnp.broadcast_to(value[None], (count,) + value.shape)
    arrived = lax.all_to_all(copies, everywhere, split_axis=0, concat_axis=0, tiled=True)
    return jnp.sum(arrived, axis=0)


def pick(value, index, axis):
    return lax.dynamic_index_in_dim(value, index, axis, keepdims=False)


def halve(value, axis, neighbour, index, token):
    sent = lax.ppermute(pick(value, 1 - index, axis), "chip", neighbour)
    if token is not None:
        sent = after(sent, token)
    kept = pick(value, index, axis).astype(jnp.float32) + sent.astype(jnp.float32)
    return kept.astype(jnp.bfloat16)


def flip(bit):
    return [(i, i ^ bit) for i in range(4)]


def chip_bits():
    index = lax.axis_index("chip")
    return lax.rem(index, 2), lax.div(index, 2)


def scatter_ring(both):
    tensor_size, index = lax.axis_size("tensor"), lax.axis_index("tensor")
    total = pick(both, index, 0).astype(jnp.float32)
    for steps in range(1, tensor_size):
        ring = [(i, (i + steps) % tensor_size) for i in range(tensor_size)]
        arrived = lax.ppermute(pick(both, lax.rem(index + steps, tensor_size), 0), "tensor", ring)
        total = total + arrived.astype(jnp.float32)
    return total


def gather_ring(block):
    tensor_size = lax.axis_size("tensor")
    blocks = [block]
    for steps in range(1, tensor_size):
        ring = [(i, (i + steps) % tensor_size) for i in range(tensor_size)]
        blocks.append(lax.ppermute(block, "tensor", ring))
    return blocks


def butterfly(value):
    for axis in ("core", "chip", "tensor"):
        count = lax.axis_size(axis)
        step = 1
        while step < count:
            value = value + lax.ppermute(value, axis, [(i, i ^ step) for i in range(count)])
            step *= 2
    return value


def norm_forward(values, gain_vec, bias_vec):
    mean_row = jnp.mean(values, axis=1, keepdims=True)
    centered = values - mean_row
    variance = jnp.mean(centered * centered, axis=1, keepdims=True)
    inv_std = lax.rsqrt(variance + norm_eps)
    normed = centered * inv_std
    return (normed, inv_std, normed * gain_vec + bias_vec)


def norm_backward(grad_normed, normed, inv_std, gain_vec):
    scaled = grad_normed * gain_vec
    plain_mean = jnp.mean(scaled, axis=1, keepdims=True)
    cross_mean = jnp.mean(scaled * normed, axis=1, keepdims=True)
    grad_values = inv_std * (scaled - plain_mean - normed * cross_mean)
    return (grad_values, jnp.sum(grad_normed * normed, axis=0), jnp.sum(grad_normed, axis=0))


def tile_of(width):
    return 384 if width % 384 == 0 else width


def attention_plan(query_pos, key_base, key_offsets, seq_ends):
    width = query_pos.shape[1]
    key_width = key_offsets.shape[0]
    tile, key_tile = tile_of(width), tile_of(key_width)
    starts = jnp.max(
        jnp.where(seq_ends[None, None, :] <= query_pos[:, :, None], seq_ends[None, None, :], 0),
        axis=2,
    )
    rows = jnp.stack((query_pos, starts), axis=1)
    tiles = query_pos.reshape(-1, tile)
    first, last = tiles[:, 0], tiles[:, tile - 1]
    last_start = starts.reshape(-1, tile)[:, tile - 1]
    offset_tiles = key_offsets.reshape(-1, key_tile)
    key_min = (key_base[:, None] + offset_tiles[None, :, 0]).reshape(-1)
    key_max = (key_base[:, None] + offset_tiles[None, :, key_tile - 1]).reshape(-1)
    key_end = jnp.min(
        jnp.where(seq_ends[None, :] > key_max[:, None], seq_ends[None, :], seq_ends[-1]), axis=1
    )
    low = jnp.sum((last[None, :] < key_min[:, None]).astype(jnp.int32), axis=1)
    high = jnp.sum((first[None, :] < key_end[:, None]).astype(jnp.int32), axis=1)
    bases = jnp.repeat(key_base, key_width // key_tile)
    plan = jnp.concatenate((low, high, bases, key_min, key_max, first, last_start))
    return (plan.astype(jnp.int32), rows.astype(jnp.int32), key_offsets[:, None].astype(jnp.int32))


def key_allowed(column_ref, rows_ref, step, per_key, key_tile, base, group, lanes):
    offset = pl.multiple_of(lax.rem(step, per_key) * key_tile, key_tile)
    key_pos = column_ref[pl.ds(offset, key_tile), :] + base
    query_pos = rows_ref[group, 0:1, lanes]
    query_start = rows_ref[group, 1:2, lanes]
    return (key_pos <= query_pos) & (key_pos >= query_start)


def forward_kernel(dims, ends, plan_ref, query_ref, pair_ref, rows_ref, column_ref, *more):
    first, final = ends
    state, more = ((), more) if first else (more[:3], more[3:])
    outs, (acc, top, tot) = more[:3], more[3:]
    blocks, groups, per_query, per_key, tile, key_tile, part = dims
    count = groups * per_query
    step = pl.program_id(0)

    @pl.when(step == 0)
    def _():
        if first:
            acc[...] = jnp.zeros_like(acc)
            top[...] = jnp.full(top.shape, masked_score, jnp.float32)
            tot[...] = jnp.zeros_like(tot)
        else:
            for held, given in zip((acc, top, tot), state):
                held[...] = given[...]

    keys = jnp.transpose(pair_ref[0, :HEAD_DIM, :].astype(jnp.float32)).astype(jnp.bfloat16)
    values_t = pair_ref[0, HEAD_DIM:, :]
    base, key_min, key_max = (plan_ref[kind * blocks + step] for kind in (2, 3, 4))

    def one_tile(index, _):
        group = lax.div(index, per_query)
        lanes = pl.ds(pl.multiple_of(lax.rem(index, per_query) * tile, tile), tile)
        queries_t = query_ref[group, :HEAD_DIM, lanes] * jnp.bfloat16(score_scale)
        inside = (key_max <= plan_ref[5 * blocks + index]) & (
            key_min >= plan_ref[5 * blocks + count + index]
        )

        def update(masked):
            scores = jnp.dot(keys, queries_t, preferred_element_type=jnp.float32)
            if masked:
                allowed = key_allowed(
                    column_ref, rows_ref, step, per_key, key_tile, base, group, lanes
                )
                scores = jnp.where(allowed, scores, masked_score)
            old_top = top[index]
            new_top = jnp.maximum(old_top, jnp.max(scores, axis=0, keepdims=True))
            weights = jnp.exp(scores - new_top)
            shrink = jnp.exp(old_top - new_top)
            top[index] = new_top
            tot[index] = tot[index] * shrink + jnp.sum(weights, axis=0, keepdims=True)
            acc[index] = acc[index] * shrink + jnp.dot(
                values_t, weights.astype(jnp.bfloat16), preferred_element_type=jnp.float32
            )

        pl.when(inside)(lambda: update(False))
        pl.when(jnp.logical_not(inside))(lambda: update(True))
        return 0

    lax.fori_loop(plan_ref[step], plan_ref[blocks + step], one_tile, 0)

    @pl.when(step == blocks - 1)
    def _():
        if not final:
            for held, given in zip(outs, (acc, top, tot)):
                held[...] = given[...]
            return
        out_ref, low_ref, total_ref = outs

        def finish(index, _):
            group = lax.div(index, per_query)
            lanes = pl.ds(pl.multiple_of(lax.rem(index, per_query) * tile, tile), tile)
            result = acc[index] / tot[index]
            out_ref[group, :, lanes] = result
            for piece in range(tile // part):
                low_ref[index * (tile // part) + piece] = result[
                    :, piece * part : (piece + 1) * part
                ].astype(jnp.bfloat16)
            total_ref[index] = top[index] + jnp.log(tot[index])
            return 0

        lax.fori_loop(0, count, finish, 0)


def backward_kernel(
    dims,
    ends,
    plan_ref,
    query_ref,
    pair_ref,
    rows_ref,
    column_ref,
    grad_ref,
    out_ref,
    total_ref,
    *more,
):
    first, final = ends
    state, more = ((), more) if first else (more[:1], more[1:])
    query_grad_ref, pair_grad_ref, acc, inner, grad_cols, query_rows, grad_rows = more[:7]
    key_acc, value_acc = more[7:]
    blocks, groups, per_query, per_key, tile, key_tile, part = dims
    count = groups * per_query
    step = pl.program_id(0)

    @pl.when(step == 0)
    def _():
        acc[...] = jnp.zeros_like(acc) if first else state[0][...]

        def prepare(index, _):
            group = lax.div(index, per_query)
            lanes = pl.ds(pl.multiple_of(lax.rem(index, per_query) * tile, tile), tile)
            for piece in range(tile // part):
                grad_cols[index, :, piece * part : (piece + 1) * part] = grad_ref[
                    index * (tile // part) + piece
                ]
            grads = grad_cols[index].astype(jnp.float32)
            inner[index] = jnp.sum(grads * out_ref[group, :, lanes], axis=0, keepdims=True)
            grad_rows[index] = jnp.transpose(grads).astype(jnp.bfloat16)
            scaled = query_ref[group, :HEAD_DIM, lanes].astype(jnp.float32) * score_scale
            query_rows[index] = jnp.transpose(scaled).astype(jnp.bfloat16)
            return 0

        lax.fori_loop(0, count, prepare, 0)

    keys_t = pair_ref[0, :HEAD_DIM, :]
    keys = jnp.transpose(keys_t.astype(jnp.float32)).astype(jnp.bfloat16)
    values = jnp.transpose(pair_ref[0, HEAD_DIM:, :].astype(jnp.float32)).astype(jnp.bfloat16)
    base, key_min, key_max = (plan_ref[kind * blocks + step] for kind in (2, 3, 4))
    key_acc[...] = jnp.zeros_like(key_acc)
    value_acc[...] = jnp.zeros_like(value_acc)

    def one_tile(index, _):
        group = lax.div(index, per_query)
        lanes = pl.ds(pl.multiple_of(lax.rem(index, per_query) * tile, tile), tile)
        queries_t = query_ref[group, :HEAD_DIM, lanes] * jnp.bfloat16(score_scale)
        grads_t = grad_cols[index]
        inside = (key_max <= plan_ref[5 * blocks + index]) & (
            key_min >= plan_ref[5 * blocks + count + index]
        )

        def update(masked):
            scores = jnp.dot(keys, queries_t, preferred_element_type=jnp.float32)
            weights = jnp.exp(scores - total_ref[index])
            if masked:
                allowed = key_allowed(
                    column_ref, rows_ref, step, per_key, key_tile, base, group, lanes
                )
                weights = jnp.where(allowed, weights, 0.0)
            grad_weights = jnp.dot(values, grads_t, preferred_element_type=jnp.float32)
            grad_scores = (weights * (grad_weights - inner[index])).astype(jnp.bfloat16)
            value_acc[...] += jnp.dot(
                weights.astype(jnp.bfloat16), grad_rows[index], preferred_element_type=jnp.float32
            )
            key_acc[...] += jnp.dot(
                grad_scores, query_rows[index], preferred_element_type=jnp.float32
            )
            acc[index] += jnp.dot(keys_t, grad_scores, preferred_element_type=jnp.float32)

        pl.when(inside)(lambda: update(False))
        pl.when(jnp.logical_not(inside))(lambda: update(True))
        return 0

    lax.fori_loop(plan_ref[step], plan_ref[blocks + step], one_tile, 0)
    pair_grad_ref[0, :HEAD_DIM, :] = jnp.transpose(key_acc[...]).astype(jnp.bfloat16)
    pair_grad_ref[0, HEAD_DIM:, :] = jnp.transpose(value_acc[...]).astype(jnp.bfloat16)

    @pl.when(step == blocks - 1)
    def _():
        if not final:
            query_grad_ref[...] = acc[...]
            return

        def finish(index, _):
            group = lax.div(index, per_query)
            lanes = pl.ds(pl.multiple_of(lax.rem(index, per_query) * tile, tile), tile)
            query_grad_ref[group, :, lanes] = (acc[index] * score_scale).astype(jnp.bfloat16)
            return 0

        lax.fori_loop(0, count, finish, 0)


def attention_call(kernel, ends, queries, pairs, plan, more, part, outs, scratch, flops):
    numbers, rows, column = plan
    groups, _, width = queries.shape
    key_groups, _, key_width = pairs.shape
    tile, key_tile = tile_of(width), tile_of(key_width)
    per_query, per_key = width // tile, key_width // key_tile
    blocks = key_groups * per_key
    count = groups * per_query

    def whole(array):
        return pl.BlockSpec(array.shape, lambda step, plan_ref: (0,) * array.ndim)

    pair_spec = pl.BlockSpec(
        (1, 2 * HEAD_DIM, key_tile),
        lambda step, plan_ref: (lax.div(step, per_key), 0, lax.rem(step, per_key)),
    )
    out_shapes, out_specs = [], []
    for kind in outs:
        if kind == "pairs":
            out_shapes.append(jax.ShapeDtypeStruct(pairs.shape, jnp.bfloat16))
            out_specs.append(pair_spec)
        else:
            shape = {
                "row": (count, 1, tile),
                "acc": (count, HEAD_DIM, tile),
                "low": (groups * width // part, HEAD_DIM, part),
            }.get(kind, (groups, HEAD_DIM, width))
            dtype = jnp.bfloat16 if kind in ("grads", "low") else jnp.float32
            out_shapes.append(jax.ShapeDtypeStruct(shape, dtype))
            out_specs.append(whole(out_shapes[-1]))
    sizes = {
        "acc": pltpu.VMEM((count, HEAD_DIM, tile), jnp.float32),
        "row": pltpu.VMEM((count, 1, tile), jnp.float32),
        "cols": pltpu.VMEM((count, HEAD_DIM, tile), jnp.bfloat16),
        "rows": pltpu.VMEM((count, tile, HEAD_DIM), jnp.bfloat16),
        "keys": pltpu.VMEM((key_tile, HEAD_DIM), jnp.float32),
    }
    pairs_near = groups * width * min(key_groups * key_width, 2304)
    return pl.pallas_call(
        functools.partial(kernel, (blocks, groups, per_query, per_key, tile, key_tile, part), ends),
        out_shape=out_shapes,
        grid_spec=pltpu.PrefetchScalarGridSpec(
            num_scalar_prefetch=1,
            grid=(blocks,),
            in_specs=[whole(queries), pair_spec, whole(rows), whole(column)]
            + [whole(array) for array in more],
            out_specs=out_specs,
            scratch_shapes=[sizes[name] for name in scratch],
        ),
        compiler_params=pltpu.CompilerParams(
            dimension_semantics=("arbitrary",), vmem_limit_bytes=56 * 2**20
        ),
        cost_estimate=pl.CostEstimate(
            flops=flops * pairs_near * HEAD_DIM,
            bytes_accessed=4 * queries.size + 4 * pairs.size,
            transcendentals=pairs_near,
        ),
    )(numbers, queries, pairs, rows, column, *more)


def attend(queries, pairs, plans, part):
    state = ()
    for index, (keys, plan) in enumerate(zip(pairs, plans)):
        ends = (index == 0, index == len(pairs) - 1)
        if index == 1:
            keys = after(keys, state)
        state = attention_call(
            forward_kernel,
            ends,
            queries,
            keys,
            plan,
            tuple(state),
            part,
            ("out", "low", "row") if ends[1] else ("acc", "row", "row"),
            ("acc", "row", "row"),
            16,
        )
    return state


def attend_back(queries, keys, plan, known, state, final):
    return attention_call(
        backward_kernel,
        (not state, final),
        queries,
        keys,
        plan,
        known + state,
        known[0].shape[2],
        ("grads" if final else "acc", "pairs"),
        ("acc", "row", "cols", "rows", "rows", "keys", "keys"),
        40,
    )


def aligned_weights(stacked, tensor_size, tensor_index, head_rows):
    slab = stacked.shape[1]
    extra = slab - head_rows
    most = (tensor_size - 1) * extra
    before = lax.ppermute(stacked[:, slab - most :], "tensor", line(tensor_size, 1))
    joined = jnp.concatenate((before, stacked), axis=1)
    own = lax.dynamic_slice_in_dim(joined, most - extra * tensor_index, head_rows, 1)
    return own


def last_weights(stacked, tensor_size, tensor_index):
    final = stacked[:, stacked.shape[1] - HEAD_DIM :]
    last = jnp.where(tensor_index == tensor_size - 1, final, jnp.zeros_like(final))
    for target in range(tensor_size - 1):
        last = last + lax.ppermute(final, "tensor", [(tensor_size - 1, target)])
    return last


def slab_rows(own, last, slab, tensor_size, tensor_index):
    extra = slab - own.shape[1]
    most = (tensor_size - 1) * extra
    following = lax.ppermute(own[:, :most], "tensor", line(tensor_size, -1))
    following = jnp.pad(following, ((0, 0), (0, HEAD_DIM - most), (0, 0)))
    following = jnp.where(tensor_index == tensor_size - 1, last, following)
    joined = jnp.concatenate((own, following), axis=1)
    return lax.dynamic_slice_in_dim(joined, extra * tensor_index, slab, 1)


def local(
    tokens_in,
    ln1_gain,
    ln1_bias,
    w_qkv,
    b_qv,
    w_out,
    b_out,
    ln2_gain,
    ln2_bias,
    w_up,
    b_up,
    w_down,
    b_down,
    seq_lengths,
    cotangent,
):
    tensor_size = lax.axis_size("tensor")
    tensor_index = lax.axis_index("tensor")
    chips = lax.axis_size("chip")
    chip_index = lax.axis_index("chip")
    core_index = lax.axis_index("core")
    dp_size = lax.axis_size(layer)
    dp_index = lax.axis_index(layer)
    flat_index = lax.axis_index(everywhere)
    devices = dp_size * tensor_size
    rows, width = tokens_in.shape
    slab = w_qkv.shape[1]
    unit_slab = w_up.shape[1]
    slots = (HEADS - 1) // tensor_size
    members = dp_size // slots
    member = lax.rem(dp_index, members)
    part = rows // members
    lanes = tensor_size * part
    head_rows = slots * HEAD_DIM
    whole_heads = width - HEAD_DIM
    low = jnp.bfloat16
    seq_ends = jnp.cumsum(seq_lengths)
    gain_one = ln1_gain.astype(jnp.float32)
    shift_one = ln1_bias.astype(jnp.float32)
    gain_two = ln2_gain.astype(jnp.float32)
    shift_two = ln2_bias.astype(jnp.float32)
    contract_first = (((0,), (0,)), ((), ()))
    contract_cols = (((1,), (1,)), ((), ()))

    stream = tokens_in.astype(jnp.float32)
    normed_one, inv_one, pre_one = norm_forward(stream, gain_one, shift_one)
    pre_one = pre_one.astype(low)
    wide_one = gather_tensor(pre_one.reshape(members, part, width), 1)
    wide_one = wide_one.reshape(members, lanes, width)
    own_w = aligned_weights(w_qkv, tensor_size, tensor_index, head_rows)
    last_w = last_weights(w_qkv, tensor_size, tensor_index)
    qkv_w = own_w.reshape(3, slots, HEAD_DIM, width).transpose(1, 0, 2, 3)
    qkv_w = qkv_w.reshape(slots, 3 * HEAD_DIM, width)
    last_qkv_w = last_w.reshape(3 * HEAD_DIM, width)
    bias_full = jnp.stack((b_qv[0], jnp.zeros_like(b_qv[0]), b_qv[1])).astype(jnp.float32)
    own_bias = lax.dynamic_slice_in_dim(bias_full, tensor_index * head_rows, head_rows, 1)
    own_bias = own_bias.reshape(3, slots, HEAD_DIM).transpose(1, 0, 2).reshape(slots, -1)
    last_bias = bias_full[:, whole_heads:].reshape(-1)

    half = unit_slab // 2
    quarter = half // chips
    if slab % chips == 0:
        out_rows = slab // chips
        out_piece = after(
            lax.dynamic_slice_in_dim(w_out, chip_index * out_rows, out_rows, 0), wide_one
        )
        full_out = lax.all_gather(out_piece, sharers, axis=0, tiled=True)
    else:
        full_out = lax.all_gather(w_out, "tensor", axis=0, tiled=True)
    unit_start = core_index * half + chip_index * quarter
    up_piece = after(lax.dynamic_slice_in_dim(w_up, unit_start, quarter, 1).T, wide_one)
    down_piece = after(lax.dynamic_slice_in_dim(w_down, unit_start, quarter, 0), wide_one)
    half_up = lax.all_gather(up_piece, sharers, axis=0, tiled=True)
    half_down = lax.all_gather(down_piece, sharers, axis=0, tiled=True)
    up_bias = lax.all_to_all(
        jnp.broadcast_to(b_up[None], (tensor_size, unit_slab)), "tensor", 0, 0, tiled=True
    )
    up_bias = lax.dynamic_slice_in_dim(up_bias, core_index * half, half, 1).reshape(-1)
    wide_grad = jnp.concatenate((cotangent, other_core(cotangent)), axis=0)

    offsets = jnp.arange(tensor_size, dtype=jnp.int32)[:, None] * rows
    offsets = (offsets + jnp.arange(part, dtype=jnp.int32)[None]).reshape(-1)
    dp_starts = jnp.arange(dp_size, dtype=jnp.int32) * (tensor_size * rows)
    query_pos = dp_starts[:, None] + offsets[None] + member * part
    halves = jnp.arange(members, dtype=jnp.int32)
    if members == 2:
        halves = lax.rem(member + halves, 2)
    key_base = halves[:, None] * part + dp_starts[None]
    bases = [key_base[0], key_base[1]] if members == 2 else [key_base.reshape(-1)]
    plans = [attention_plan(query_pos, base, offsets, seq_ends) for base in bases]
    row_range = jnp.arange(rows, dtype=jnp.int32)
    steps_back = min(-(-REACH // tensor_size), dp_size - 1) + 1
    last_base = dp_index - jnp.arange(steps_back, dtype=jnp.int32)
    distance = tensor_index + tensor_size - jnp.arange(tensor_size, dtype=jnp.int32)
    last_base = last_base[None] * tensor_size + lax.rem(distance, tensor_size)[:, None]
    last_base = last_base.reshape(-1) * rows
    last_plan = attention_plan(
        (flat_index * rows + row_range)[None], last_base, row_range, seq_ends
    )

    qkv = jnp.einsum("cfd,gtd->cgft", qkv_w, wide_one, preferred_element_type=jnp.float32)
    qkv = (qkv + own_bias[:, None, :, None]).astype(low).reshape(dp_size, 3 * HEAD_DIM, lanes)
    qkv = lax.all_to_all(qkv, layer, split_axis=0, concat_axis=0, tiled=True)
    last_qkv = jnp.einsum("fd,td->ft", last_qkv_w, pre_one, preferred_element_type=jnp.float32)
    last_qkv = (last_qkv + last_bias[:, None]).astype(low)[None]
    own_pairs = qkv[:, HEAD_DIM:]
    last_pairs = last_qkv[:, HEAD_DIM:]
    last_pairs = [last_pairs] + [
        lax.ppermute(last_pairs, layer, line(dp_size, step)) for step in range(1, steps_back)
    ]
    last_blocks = gather_ring(jnp.concatenate(last_pairs, axis=0))
    sharing = [list(range(i, i + members)) for i in range(0, dp_size, members)]
    if members == 2:
        pairs = [own_pairs, other_core(own_pairs)]
    else:
        pairs = [lax.all_gather(own_pairs, layer, axis_index_groups=sharing, axis=0, tiled=True)]
    mixed, mixed_low, total = attend(qkv, pairs, plans, part)
    attended = lax.all_to_all(mixed_low, everywhere, split_axis=0, concat_axis=0, tiled=True)
    last_pairs = jnp.concatenate(after(last_blocks, total), axis=0)
    last_mixed, last_low, last_total = attend(
        after(last_qkv, total), [last_pairs], [last_plan], rows
    )

    attended = attended.reshape(slots, members, tensor_size, HEAD_DIM, part)
    attended = attended.transpose(1, 2, 0, 3, 4).reshape(members, whole_heads, part)
    branch = jnp.einsum(
        "gkt,kd->gtd", attended, full_out[:whole_heads], preferred_element_type=jnp.float32
    ).reshape(rows, width)
    branch = branch + lax.dot_general(
        last_low[0], full_out[whole_heads:], contract_first, preferred_element_type=jnp.float32
    )
    stream_one = stream + branch + b_out.astype(jnp.float32)
    normed_two, inv_two, pre_two = norm_forward(stream_one, gain_two, shift_two)
    pre_two = pre_two.astype(low)
    wide_two = jnp.concatenate((pre_two, other_core(pre_two)), axis=0)
    hidden_pre = lax.dot_general(
        wide_two, half_up, contract_cols, preferred_element_type=jnp.float32
    ) + up_bias.astype(jnp.float32)
    gelu_out, gelu_pull = jax.vjp(
        lambda hidden_in: jax.nn.gelu(hidden_in, approximate=True), hidden_pre
    )
    activated = gelu_out.astype(low)
    grad_act = lax.dot_general(
        wide_grad, half_down, contract_cols, preferred_element_type=jnp.float32
    )
    grad_hidden = gelu_pull(grad_act)[0].astype(low)
    grad_up_part = jnp.sum(grad_hidden.astype(jnp.float32), axis=0)
    grad_two = cotangent.astype(jnp.float32)
    grad_down_bias = jnp.sum(grad_two, axis=0)
    grad_normed_two = jnp.dot(grad_hidden, half_up, preferred_element_type=jnp.float32)
    grad_normed_two = grad_normed_two[:rows] + other_core(
        grad_normed_two[rows:].astype(low)
    ).astype(jnp.float32)
    down_sum = jnp.dot(activated, half_down, preferred_element_type=jnp.float32)
    down_sum = down_sum[:rows] + other_core(down_sum[rows:].astype(low)).astype(jnp.float32)
    block_out = (stream_one + down_sum + b_down.astype(jnp.float32)).astype(low)
    grad_res_two, grad_gain_two, grad_shift_two = norm_backward(
        grad_normed_two, normed_two, inv_two, gain_two
    )
    grad_stream_one = grad_two + grad_res_two
    grad_branch = grad_stream_one.astype(low)
    grad_out_bias = jnp.sum(grad_branch.astype(jnp.float32), axis=0)

    branch_parts = grad_branch.reshape(members, part, width)
    grads = jnp.einsum(
        "kd,gtd->gkt", full_out[:whole_heads], branch_parts, preferred_element_type=jnp.float32
    )
    grads = grads.astype(low).reshape(members, tensor_size, slots, HEAD_DIM, part)
    grads = grads.transpose(2, 0, 1, 3, 4).reshape(devices, HEAD_DIM, part)
    grads = lax.all_to_all(grads, everywhere, split_axis=0, concat_axis=0, tiled=True)
    last_grads = lax.dot_general(
        full_out[whole_heads:], grad_branch, contract_cols, preferred_element_type=jnp.float32
    )
    last_grads = last_grads.astype(low)[None]
    last_query_grad, last_pair_grad = attend_back(
        last_qkv, last_pairs, last_plan, (last_grads, last_mixed, last_total), (), True
    )
    column = width // dp_size
    grad_down = lax.dot_general(
        wide_grad, activated, contract_first, preferred_element_type=jnp.float32
    ).astype(low)
    grad_up = lax.dot_general(
        wide_two, grad_hidden, contract_first, preferred_element_type=jnp.float32
    ).astype(low)
    grad_out = jnp.einsum(
        "gtd,gkt->dk", branch_parts, attended, preferred_element_type=jnp.float32
    )
    last_out = lax.dot_general(
        grad_branch, last_low[0], (((0,), (1,)), ((), ())), preferred_element_type=jnp.float32
    )
    grad_out = jnp.concatenate((grad_out, last_out), axis=1).astype(low)
    low_bit, high_bit = chip_bits()
    if chips != 4:
        grad_down = lax.psum_scatter(grad_down, "chip", scatter_dimension=0, tiled=True)
        grad_up = lax.psum_scatter(grad_up, "chip", scatter_dimension=0, tiled=True)
        grad_out = lax.psum_scatter(grad_out, "chip", scatter_dimension=0, tiled=True)
    last_pair_grad = last_pair_grad.reshape(tensor_size, steps_back, 2 * HEAD_DIM, rows)
    last_arrived = [last_pair_grad[0]]
    for step in range(1, tensor_size):
        back = [(i, (i - step) % tensor_size) for i in range(tensor_size)]
        last_arrived.append(lax.ppermute(last_pair_grad[step], "tensor", back))
    known = (grads, mixed, total)
    if members == 2:
        query_state, pair_grad = attend_back(qkv, pairs[1], plans[1], known, (), False)
        other_grad = other_core(pair_grad)
        last_arrived = after(last_arrived, query_state)
        last_arrived = sum(block.astype(jnp.float32) for block in last_arrived)
        last_blocks = [
            lax.ppermute(last_arrived[step].astype(low), layer, line(dp_size, -step))
            for step in range(1, steps_back)
        ]
        if chips == 4:
            blocked = (2, 2, 2 * column, -1)
            grad_down = halve(grad_down.reshape(blocked), 0, flip(2), high_bit, query_state)
            grad_up = halve(grad_up.reshape(blocked), 1, flip(1), low_bit, query_state)
            grad_out = halve(grad_out.reshape(blocked), 1, flip(1), low_bit, query_state)
        query_grad, pair_grad = attend_back(
            qkv, pairs[0], plans[0], known, (query_state,), True
        )
        if chips == 4:
            grad_down = halve(grad_down, 0, flip(1), low_bit, query_grad)
            grad_up = halve(grad_up, 0, flip(2), high_bit, query_grad)
            grad_out = halve(grad_out, 0, flip(2), high_bit, query_grad)
        last_sum = last_arrived[0]
        for block in after(last_blocks, query_grad):
            last_sum = last_sum + block.astype(jnp.float32)
        pair_sum = pair_grad.astype(jnp.float32) + other_grad.astype(jnp.float32)
    else:
        last_arrived = sum(block.astype(jnp.float32) for block in last_arrived)
        last_sum = last_arrived[0]
        for step in range(1, steps_back):
            arrived = lax.ppermute(last_arrived[step].astype(low), layer, line(dp_size, -step))
            last_sum = last_sum + arrived.astype(jnp.float32)
        query_grad, pair_grad = attend_back(qkv, pairs[0], plans[0], known, (), True)
        pair_grad = pair_grad.reshape(members, dp_size, 2 * HEAD_DIM, lanes)
        pair_grad = lax.all_to_all(pair_grad, layer, 0, 0, axis_index_groups=sharing, tiled=True)
        pair_sum = jnp.sum(pair_grad.astype(jnp.float32), axis=0)
    last_pair_grad = last_sum.astype(low)
    qkv_grad = jnp.concatenate((query_grad, pair_sum.astype(low)), axis=1)
    qkv_grad = lax.all_to_all(qkv_grad, layer, split_axis=0, concat_axis=0, tiled=True)
    qkv_grad = qkv_grad.reshape(slots, members, 3 * HEAD_DIM, lanes)
    last_qkv_grad = jnp.concatenate((last_query_grad[0], last_pair_grad), axis=0)

    grad_normed_one = []
    for piece in range(members):
        product = jnp.einsum(
            "cfd,cft->dt", qkv_w, qkv_grad[:, piece], preferred_element_type=jnp.float32
        )
        product = product.astype(low).T.reshape(tensor_size, part, width)
        grad_normed_one.append(scatter_tensor(product))
    grad_normed_one = jnp.concatenate(grad_normed_one, axis=0)
    last_normed_one = lax.dot_general(
        last_qkv_grad, last_qkv_w, contract_first, preferred_element_type=jnp.float32
    )
    grad_normed_one = grad_normed_one + last_normed_one
    grad_res_one, grad_gain_one, grad_shift_one = norm_backward(
        grad_normed_one, normed_one, inv_one, gain_one
    )
    grad_input = grad_stream_one + grad_res_one

    units = jnp.stack((grad_up, grad_down)).reshape(2, 2 * column, tensor_size, half)
    units = scatter_ring(units.transpose(2, 0, 1, 3))
    units = units.astype(low).reshape(2, 2, column, half)
    kept = pick(units, core_index, 1)
    arrived = other_core(pick(units, 1 - core_index, 1))
    units = (
        jnp.where(core_index == 0, kept, arrived),
        jnp.where(core_index == 0, arrived, kept),
    )
    units = jnp.concatenate(units, axis=2).astype(jnp.float32)
    grad_out = grad_out.reshape(2 * column, tensor_size, slab).transpose(1, 0, 2)
    grad_out = scatter_ring(grad_out).reshape(2, column, slab)
    sent = other_core(pick(grad_out, 1 - core_index, 0).astype(low))
    grad_out = (pick(grad_out, core_index, 0) + sent.astype(jnp.float32)).T

    own_qkv_grad = jnp.einsum(
        "gtd,cgft->dcf", wide_one, qkv_grad, preferred_element_type=jnp.float32
    )
    last_part = lax.dot_general(
        pre_one, last_qkv_grad, (((0,), (1,)), ((), ())), preferred_element_type=jnp.float32
    )
    grad_qkv = jnp.concatenate((own_qkv_grad.reshape(width, -1), last_part), axis=1).astype(low)
    if chips == 4:
        grad_qkv = grad_qkv.reshape(2, 2, 2, column, -1)
        sent = other_core(pick(grad_qkv, 1 - core_index, 2))
        kept = pick(grad_qkv, core_index, 2).astype(jnp.float32)
        grad_qkv = (kept + sent.astype(jnp.float32)).astype(low)
        grad_qkv = halve(grad_qkv, 1, flip(1), low_bit, None)
        grad_qkv = halve(grad_qkv, 0, flip(2), high_bit, None)
    else:
        grad_qkv = lax.psum_scatter(grad_qkv, layer, scatter_dimension=0, tiled=True)
    own_qkv_grad = grad_qkv[:, : 3 * head_rows].T.reshape(slots, 3, HEAD_DIM, column)
    own_qkv_grad = own_qkv_grad.transpose(1, 0, 2, 3).reshape(3, head_rows, column)
    last_part = grad_qkv[:, 3 * head_rows :].T.reshape(3, HEAD_DIM, column)
    last_sum = last_part.astype(jnp.float32)
    for source in range(tensor_size - 1):
        arrived = lax.ppermute(last_part, "tensor", [(source, tensor_size - 1)])
        last_sum = last_sum + arrived.astype(jnp.float32)
    grad_qkv = slab_rows(own_qkv_grad, last_sum.astype(low), slab, tensor_size, tensor_index)
    grad_qkv = grad_qkv.astype(jnp.float32)

    head = tensor_index * slots + lax.div(dp_index, members)
    own_sums = (jnp.sum(query_grad.astype(jnp.float32), axis=(0, 2)),)
    own_sums += (jnp.sum(pair_sum[:, HEAD_DIM:], axis=(0, 2)),)
    last_sums = jnp.sum(last_qkv_grad.astype(jnp.float32), axis=1).reshape(3, HEAD_DIM)
    qv_sum = jnp.zeros((2, HEADS, HEAD_DIM), jnp.float32).at[:, HEADS - 1].set(last_sums[::2])
    qv_sum = lax.dynamic_update_slice_in_dim(qv_sum, jnp.stack(own_sums)[:, None], head, 1)
    up_full = lax.dynamic_update_slice_in_dim(
        jnp.zeros((tensor_size, unit_slab), jnp.float32),
        grad_up_part.reshape(tensor_size, half),
        core_index * half,
        1,
    ).reshape(-1)
    early = jnp.concatenate(
        (grad_out_bias, grad_gain_two, grad_shift_two, grad_down_bias, up_full, qv_sum.reshape(-1))
    )
    early = butterfly(early)
    qv_sum = early[-2 * width :].reshape(2, width)
    early, up_sum = early[: 4 * width].reshape(4, width), early[4 * width : -2 * width]
    late = small_sum(jnp.stack((grad_gain_one, grad_shift_one)))
    grad_up_bias = lax.dynamic_slice_in_dim(up_sum, tensor_index * unit_slab, unit_slab, 0)
    return (
        block_out,
        grad_input,
        late[0],
        late[1],
        grad_qkv,
        qv_sum,
        grad_out,
        early[0],
        early[1],
        early[2],
        units[0],
        grad_up_bias,
        units[1].T,
        early[3],
    )


def solution(mesh):
    chips, tensor = mesh.shape["dp"] // 2, mesh.shape["tensor"]
    cores = jax.sharding.Mesh(mesh.devices.reshape(chips, 2, tensor), everywhere)
    in_specs = (
        P(everywhere, None),
        P(),
        P(),
        P(None, "tensor", None),
        P(),
        P("tensor", None),
        P(),
        P(),
        P(),
        P(None, "tensor"),
        P("tensor"),
        P("tensor", None),
        P(),
        P(),
        P(everywhere, None),
    )
    out_specs = (
        P(everywhere, None),
        P(everywhere, None),
        P(),
        P(),
        P(None, "tensor", layer),
        P(),
        P("tensor", layer),
        P(),
        P(),
        P(),
        P(layer, "tensor"),
        P("tensor"),
        P("tensor", layer),
        P(),
    )
    return jax.shard_map(local, mesh=cores, in_specs=in_specs, out_specs=out_specs, check_vma=False)
```

```python
import jax
import jax.numpy as jnp
from jax import lax
from jax.experimental import pallas as pl
from jax.experimental.pallas import tpu as pltpu
from jax.sharding import PartitionSpec as P

HEADS = 17
HEAD_DIM = 64
REACH = 11

norm_eps = 1e-05
score_scale = 0.125
masked_score = -1e30
everywhere = ("chip", "core", "tensor")
layer = ("chip", "core")
sharers = ("tensor", "chip")


def line(count, steps):
    first, last = (max(0, -steps), min(count, count - steps))
    return [(source, source + steps) for source in range(first, last)]


def gather_tensor(rows, axis):
    count = lax.axis_size("tensor")
    index = lax.axis_index("tensor")
    up, down = [rows], [rows]
    for _ in range(count - 1):
        up.append(lax.ppermute(up[-1], "tensor", line(count, 1)))
        down.append(lax.ppermute(down[-1], "tensor", line(count, -1)))
    shape = rows.shape[:axis] + (count,) + rows.shape[axis:]
    gathered = lax.dynamic_update_index_in_dim(jnp.zeros(shape, rows.dtype), rows, index, axis)
    for steps in range(1, count):
        block = jnp.where(index >= steps, up[steps], down[count - steps])
        gathered = lax.dynamic_update_index_in_dim(
            gathered, block, lax.rem(index - steps + count, count), axis
        )
    return gathered


def scatter_tensor(partial_sum):
    arrived = lax.all_to_all(partial_sum, "tensor", split_axis=0, concat_axis=0, tiled=True)
    return jnp.sum(arrived.astype(jnp.float32), axis=0)


def after(value, token):
    return lax.optimization_barrier((value, token))[0]


def other_core(value):
    return lax.ppermute(value, "core", [(0, 1), (1, 0)])


def small_sum(value):
    count = lax.axis_size(everywhere)
    copies = jnp.broadcast_to(value[None], (count,) + value.shape)
    arrived = lax.all_to_all(copies, everywhere, split_axis=0, concat_axis=0, tiled=True)
    return jnp.sum(arrived, axis=0)


def nothing(value):
    return jnp.minimum(jnp.abs(value[(0,) * value.ndim].astype(jnp.float32)), 0.0)


def pick(value, index, axis):
    return lax.dynamic_index_in_dim(value, index, axis, keepdims=False)


def halve(value, axis, neighbour, index, token):
    sent = lax.ppermute(pick(value, 1 - index, axis), "chip", neighbour)
    if token is not None:
        sent = after(sent, token)
    kept = pick(value, index, axis).astype(jnp.float32) + sent.astype(jnp.float32)
    return kept.astype(jnp.bfloat16)


def flip(bit):
    return [(i, i ^ bit) for i in range(4)]


def chip_bits():
    index = lax.axis_index("chip")
    return lax.rem(index, 2), lax.div(index, 2)


def scatter_ring(both):
    tensor_size, index = lax.axis_size("tensor"), lax.axis_index("tensor")
    total = pick(both, index, 0).astype(jnp.float32)
    for steps in range(1, tensor_size):
        ring = [(i, (i + steps) % tensor_size) for i in range(tensor_size)]
        arrived = lax.ppermute(pick(both, lax.rem(index + steps, tensor_size), 0), "tensor", ring)
        total = total + arrived.astype(jnp.float32)
    return total


def gather_ring(block):
    tensor_size = lax.axis_size("tensor")
    blocks = [block]
    for steps in range(1, tensor_size):
        ring = [(i, (i + steps) % tensor_size) for i in range(tensor_size)]
        blocks.append(lax.ppermute(block, "tensor", ring))
    return blocks


def butterfly(value):
    for axis in ("core", "chip", "tensor"):
        count = lax.axis_size(axis)
        step = 1
        while step < count:
            value = value + lax.ppermute(value, axis, [(i, i ^ step) for i in range(count)])
            step *= 2
    return value


def norm_forward(values, gain_vec, bias_vec):
    mean_row = jnp.mean(values, axis=1, keepdims=True)
    centered = values - mean_row
    variance = jnp.mean(centered * centered, axis=1, keepdims=True)
    inv_std = lax.rsqrt(variance + norm_eps)
    normed = centered * inv_std
    return (normed, inv_std, normed * gain_vec + bias_vec)


def norm_backward(grad_normed, normed, inv_std, gain_vec):
    scaled = grad_normed * gain_vec
    plain_mean = jnp.mean(scaled, axis=1, keepdims=True)
    cross_mean = jnp.mean(scaled * normed, axis=1, keepdims=True)
    grad_values = inv_std * (scaled - plain_mean - normed * cross_mean)
    return (grad_values, jnp.sum(grad_normed * normed, axis=0), jnp.sum(grad_normed, axis=0))


def tile_of(width):
    return 384 if width % 384 == 0 else width


def attention_plan(query_pos, key_base, key_offsets, seq_ends):
    width = query_pos.shape[1]
    key_width = key_offsets.shape[0]
    tile, key_tile = tile_of(width), tile_of(key_width)
    starts = jnp.max(
        jnp.where(seq_ends[None, None, :] <= query_pos[:, :, None], seq_ends[None, None, :], 0),
        axis=2,
    )
    rows = jnp.stack((query_pos, starts), axis=1)
    tiles = query_pos.reshape(-1, tile)
    first, last = tiles[:, 0], tiles[:, tile - 1]
    last_start = starts.reshape(-1, tile)[:, tile - 1]
    offset_tiles = key_offsets.reshape(-1, key_tile)
    key_min = (key_base[:, None] + offset_tiles[None, :, 0]).reshape(-1)
    key_max = (key_base[:, None] + offset_tiles[None, :, key_tile - 1]).reshape(-1)
    key_end = jnp.min(
        jnp.where(seq_ends[None, :] > key_max[:, None], seq_ends[None, :], seq_ends[-1]), axis=1
    )
    low = jnp.sum((last[None, :] < key_min[:, None]).astype(jnp.int32), axis=1)
    high = jnp.sum((first[None, :] < key_end[:, None]).astype(jnp.int32), axis=1)
    bases = jnp.repeat(key_base, key_width // key_tile)
    plan = jnp.concatenate((low, high, bases, key_min, key_max, first, last_start))
    return (plan.astype(jnp.int32), rows.astype(jnp.int32), key_offsets[:, None].astype(jnp.int32))


def key_allowed(column_ref, rows_ref, step, per_key, key_tile, base, group, lanes):
    offset = pl.multiple_of(lax.rem(step, per_key) * key_tile, key_tile)
    key_pos = column_ref[pl.ds(offset, key_tile), :] + base
    query_pos = rows_ref[group, 0:1, lanes]
    query_start = rows_ref[group, 1:2, lanes]
    return (key_pos <= query_pos) & (key_pos >= query_start)


def forward_kernel(dims, ends, plan_ref, query_ref, pair_ref, rows_ref, column_ref, *more):
    first, final = ends
    state, more = ((), more) if first else (more[:3], more[3:])
    outs, (acc, top, tot) = more[:3], more[3:]
    blocks, groups, per_query, per_key, tile, key_tile, part = dims
    count = groups * per_query
    step = pl.program_id(0)

    @pl.when(step == 0)
    def _():
        if first:
            acc[...] = jnp.zeros_like(acc)
            top[...] = jnp.full(top.shape, masked_score, jnp.float32)
            tot[...] = jnp.zeros_like(tot)
        else:
            for held, given in zip((acc, top, tot), state):
                held[...] = given[...]

    keys = jnp.transpose(pair_ref[0, :HEAD_DIM, :].astype(jnp.float32)).astype(jnp.bfloat16)
    values_t = pair_ref[0, HEAD_DIM:, :]
    base, key_min, key_max = (plan_ref[kind * blocks + step] for kind in (2, 3, 4))

    def one_tile(index, _):
        group = lax.div(index, per_query)
        lanes = pl.ds(pl.multiple_of(lax.rem(index, per_query) * tile, tile), tile)
        queries_t = query_ref[group, :HEAD_DIM, lanes] * jnp.bfloat16(score_scale)
        inside = (key_max <= plan_ref[5 * blocks + index]) & (
            key_min >= plan_ref[5 * blocks + count + index]
        )

        def update(masked):
            scores = jnp.dot(keys, queries_t, preferred_element_type=jnp.float32)
            if masked:
                allowed = key_allowed(
                    column_ref, rows_ref, step, per_key, key_tile, base, group, lanes
                )
                scores = jnp.where(allowed, scores, masked_score)
            old_top = top[index]
            new_top = jnp.maximum(old_top, jnp.max(scores, axis=0, keepdims=True))
            weights = jnp.exp(scores - new_top)
            shrink = jnp.exp(old_top - new_top)
            top[index] = new_top
            tot[index] = tot[index] * shrink + jnp.sum(weights, axis=0, keepdims=True)
            acc[index] = acc[index] * shrink + jnp.dot(
                values_t, weights.astype(jnp.bfloat16), preferred_element_type=jnp.float32
            )

        pl.when(inside)(lambda: update(False))
        pl.when(jnp.logical_not(inside))(lambda: update(True))
        return 0

    lax.fori_loop(plan_ref[step], plan_ref[blocks + step], one_tile, 0)

    @pl.when(step == blocks - 1)
    def _():
        if not final:
            for held, given in zip(outs, (acc, top, tot)):
                held[...] = given[...]
            return
        out_ref, low_ref, total_ref = outs

        def finish(index, _):
            group = lax.div(index, per_query)
            lanes = pl.ds(pl.multiple_of(lax.rem(index, per_query) * tile, tile), tile)
            result = acc[index] / tot[index]
            out_ref[group, :, lanes] = result
            for piece in range(tile // part):
                low_ref[index * (tile // part) + piece] = result[
                    :, piece * part : (piece + 1) * part
                ].astype(jnp.bfloat16)
            total_ref[index] = top[index] + jnp.log(tot[index])
            return 0

        lax.fori_loop(0, count, finish, 0)


def backward_kernel(
    dims,
    ends,
    plan_ref,
    query_ref,
    pair_ref,
    rows_ref,
    column_ref,
    grad_ref,
    out_ref,
    total_ref,
    *more,
):
    first, final = ends
    state, more = ((), more) if first else (more[:1], more[1:])
    query_grad_ref, pair_grad_ref, acc, inner, grad_cols, query_rows, grad_rows = more[:7]
    key_acc, value_acc = more[7:]
    blocks, groups, per_query, per_key, tile, key_tile, part = dims
    count = groups * per_query
    step = pl.program_id(0)

    @pl.when(step == 0)
    def _():
        acc[...] = jnp.zeros_like(acc) if first else state[0][...]

        def prepare(index, _):
            group = lax.div(index, per_query)
            lanes = pl.ds(pl.multiple_of(lax.rem(index, per_query) * tile, tile), tile)
            for piece in range(tile // part):
                grad_cols[index, :, piece * part : (piece + 1) * part] = grad_ref[
                    index * (tile // part) + piece
                ]
            grads = grad_cols[index].astype(jnp.float32)
            inner[index] = jnp.sum(grads * out_ref[group, :, lanes], axis=0, keepdims=True)
            grad_rows[index] = jnp.transpose(grads).astype(jnp.bfloat16)
            scaled = query_ref[group, :HEAD_DIM, lanes].astype(jnp.float32) * score_scale
            query_rows[index] = jnp.transpose(scaled).astype(jnp.bfloat16)
            return 0

        lax.fori_loop(0, count, prepare, 0)

    keys_t = pair_ref[0, :HEAD_DIM, :]
    keys = jnp.transpose(keys_t.astype(jnp.float32)).astype(jnp.bfloat16)
    values = jnp.transpose(pair_ref[0, HEAD_DIM:, :].astype(jnp.float32)).astype(jnp.bfloat16)
    base, key_min, key_max = (plan_ref[kind * blocks + step] for kind in (2, 3, 4))
    key_acc[...] = jnp.zeros_like(key_acc)
    value_acc[...] = jnp.zeros_like(value_acc)

    def one_tile(index, _):
        group = lax.div(index, per_query)
        lanes = pl.ds(pl.multiple_of(lax.rem(index, per_query) * tile, tile), tile)
        queries_t = query_ref[group, :HEAD_DIM, lanes] * jnp.bfloat16(score_scale)
        grads_t = grad_cols[index]
        inside = (key_max <= plan_ref[5 * blocks + index]) & (
            key_min >= plan_ref[5 * blocks + count + index]
        )

        def update(masked):
            scores = jnp.dot(keys, queries_t, preferred_element_type=jnp.float32)
            weights = jnp.exp(scores - total_ref[index])
            if masked:
                allowed = key_allowed(
                    column_ref, rows_ref, step, per_key, key_tile, base, group, lanes
                )
                weights = jnp.where(allowed, weights, 0.0)
            grad_weights = jnp.dot(values, grads_t, preferred_element_type=jnp.float32)
            grad_scores = (weights * (grad_weights - inner[index])).astype(jnp.bfloat16)
            value_acc[...] += jnp.dot(
                weights.astype(jnp.bfloat16), grad_rows[index], preferred_element_type=jnp.float32
            )
            key_acc[...] += jnp.dot(
                grad_scores, query_rows[index], preferred_element_type=jnp.float32
            )
            acc[index] += jnp.dot(keys_t, grad_scores, preferred_element_type=jnp.float32)

        pl.when(inside)(lambda: update(False))
        pl.when(jnp.logical_not(inside))(lambda: update(True))
        return 0

    lax.fori_loop(plan_ref[step], plan_ref[blocks + step], one_tile, 0)
    pair_grad_ref[0, :HEAD_DIM, :] = jnp.transpose(key_acc[...]).astype(jnp.bfloat16)
    pair_grad_ref[0, HEAD_DIM:, :] = jnp.transpose(value_acc[...]).astype(jnp.bfloat16)

    @pl.when(step == blocks - 1)
    def _():
        if not final:
            query_grad_ref[...] = acc[...]
            return

        def finish(index, _):
            group = lax.div(index, per_query)
            lanes = pl.ds(pl.multiple_of(lax.rem(index, per_query) * tile, tile), tile)
            query_grad_ref[group, :, lanes] = (acc[index] * score_scale).astype(jnp.bfloat16)
            return 0

        lax.fori_loop(0, count, finish, 0)


def attention_call(kernel, ends, queries, pairs, plan, more, part, outs, scratch, flops, tokens):
    numbers, rows, column = plan
    groups, _, width = queries.shape
    key_groups, _, key_width = pairs.shape
    tile, key_tile = tile_of(width), tile_of(key_width)
    per_query, per_key = width // tile, key_width // key_tile
    blocks = key_groups * per_key
    count = groups * per_query

    def whole(array):
        return pl.BlockSpec(array.shape, lambda step, plan_ref: (0,) * array.ndim)

    pair_spec = pl.BlockSpec(
        (1, 2 * HEAD_DIM, key_tile),
        lambda step, plan_ref: (lax.div(step, per_key), 0, lax.rem(step, per_key)),
    )
    out_shapes, out_specs = [], []
    for kind in outs:
        if kind == "pairs":
            out_shapes.append(jax.ShapeDtypeStruct(pairs.shape, jnp.bfloat16))
            out_specs.append(pair_spec)
        else:
            shape = {
                "row": (count, 1, tile),
                "acc": (count, HEAD_DIM, tile),
                "low": (groups * width // part, HEAD_DIM, part),
            }.get(kind, (groups, HEAD_DIM, width))
            dtype = jnp.bfloat16 if kind in ("grads", "low") else jnp.float32
            out_shapes.append(jax.ShapeDtypeStruct(shape, dtype))
            out_specs.append(whole(out_shapes[-1]))
    sizes = {
        "acc": pltpu.VMEM((count, HEAD_DIM, tile), jnp.float32),
        "row": pltpu.VMEM((count, 1, tile), jnp.float32),
        "cols": pltpu.VMEM((count, HEAD_DIM, tile), jnp.bfloat16),
        "rows": pltpu.VMEM((count, tile, HEAD_DIM), jnp.bfloat16),
        "keys": pltpu.VMEM((key_tile, HEAD_DIM), jnp.float32),
    }
    position = 5 + len(more)

    def body(*refs):
        kernel(dims, ends, *refs[:position], *refs[position + len(tokens) :])

    dims = (blocks, groups, per_query, per_key, tile, key_tile, part)
    pairs_near = groups * width * min(key_groups * key_width, 2304)
    return pl.pallas_call(
        body,
        out_shape=out_shapes,
        grid_spec=pltpu.PrefetchScalarGridSpec(
            num_scalar_prefetch=1,
            grid=(blocks,),
            in_specs=[whole(queries), pair_spec, whole(rows), whole(column)]
            + [whole(array) for array in more]
            + [pl.BlockSpec(memory_space=pl.ANY)] * len(tokens),
            out_specs=out_specs,
            scratch_shapes=[sizes[name] for name in scratch],
        ),
        compiler_params=pltpu.CompilerParams(
            dimension_semantics=("arbitrary",), vmem_limit_bytes=56 * 2**20
        ),
        cost_estimate=pl.CostEstimate(
            flops=flops * pairs_near * HEAD_DIM,
            bytes_accessed=4 * queries.size + 4 * pairs.size,
            transcendentals=pairs_near,
        ),
    )(numbers, queries, pairs, rows, column, *more, *tokens)


def attend(queries, pairs, plans, part, tokens):
    state = ()
    for index, (keys, plan) in enumerate(zip(pairs, plans)):
        ends = (index == 0, index == len(pairs) - 1)
        if index == 1:
            keys = after(keys, state)
        state = attention_call(
            forward_kernel,
            ends,
            queries,
            keys,
            plan,
            tuple(state),
            part,
            ("out", "low", "row") if ends[1] else ("acc", "row", "row"),
            ("acc", "row", "row"),
            16,
            tuple(tokens) if ends[1] else (),
        )
    return state


def attend_back(queries, keys, plan, known, state, final, tokens):
    return attention_call(
        backward_kernel,
        (not state, final),
        queries,
        keys,
        plan,
        known + state,
        known[0].shape[2],
        ("grads" if final else "acc", "pairs"),
        ("acc", "row", "cols", "rows", "rows", "keys", "keys"),
        40,
        tokens,
    )


def aligned_weights(stacked, tensor_size, tensor_index, head_rows):
    slab = stacked.shape[1]
    extra = slab - head_rows
    most = (tensor_size - 1) * extra
    before = lax.ppermute(stacked[:, slab - most :], "tensor", line(tensor_size, 1))
    joined = jnp.concatenate((before, stacked), axis=1)
    own = lax.dynamic_slice_in_dim(joined, most - extra * tensor_index, head_rows, 1)
    return own


def last_weights(stacked, tensor_size, tensor_index):
    final = stacked[:, stacked.shape[1] - HEAD_DIM :]
    last = jnp.where(tensor_index == tensor_size - 1, final, jnp.zeros_like(final))
    for target in range(tensor_size - 1):
        last = last + lax.ppermute(final, "tensor", [(tensor_size - 1, target)])
    return last


def slab_rows(own, last, slab, tensor_size, tensor_index):
    extra = slab - own.shape[1]
    most = (tensor_size - 1) * extra
    following = lax.ppermute(own[:, :most], "tensor", line(tensor_size, -1))
    following = jnp.pad(following, ((0, 0), (0, HEAD_DIM - most), (0, 0)))
    following = jnp.where(tensor_index == tensor_size - 1, last, following)
    joined = jnp.concatenate((own, following), axis=1)
    return lax.dynamic_slice_in_dim(joined, extra * tensor_index, slab, 1)


def local(
    tokens_in,
    ln1_gain,
    ln1_bias,
    w_qkv,
    b_qv,
    w_out,
    b_out,
    ln2_gain,
    ln2_bias,
    w_up,
    b_up,
    w_down,
    b_down,
    seq_lengths,
    cotangent,
):
    tensor_size = lax.axis_size("tensor")
    tensor_index = lax.axis_index("tensor")
    chips = lax.axis_size("chip")
    chip_index = lax.axis_index("chip")
    core_index = lax.axis_index("core")
    dp_size = lax.axis_size(layer)
    dp_index = lax.axis_index(layer)
    flat_index = lax.axis_index(everywhere)
    devices = dp_size * tensor_size
    rows, width = tokens_in.shape
    slab = w_qkv.shape[1]
    unit_slab = w_up.shape[1]
    slots = (HEADS - 1) // tensor_size
    members = dp_size // slots
    member = lax.rem(dp_index, members)
    part = rows // members
    lanes = tensor_size * part
    head_rows = slots * HEAD_DIM
    whole_heads = width - HEAD_DIM
    low = jnp.bfloat16
    seq_ends = jnp.cumsum(seq_lengths)
    gain_one = ln1_gain.astype(jnp.float32)
    shift_one = ln1_bias.astype(jnp.float32)
    gain_two = ln2_gain.astype(jnp.float32)
    shift_two = ln2_bias.astype(jnp.float32)
    contract_first = (((0,), (0,)), ((), ()))
    contract_cols = (((1,), (1,)), ((), ()))

    stream = tokens_in.astype(jnp.float32)
    normed_one, inv_one, pre_one = norm_forward(stream, gain_one, shift_one)
    pre_one = pre_one.astype(low)
    wide_one = gather_tensor(pre_one.reshape(members, part, width), 1)
    wide_one = wide_one.reshape(members, lanes, width)
    own_w = aligned_weights(w_qkv, tensor_size, tensor_index, head_rows)
    last_w = last_weights(w_qkv, tensor_size, tensor_index)
    qkv_w = own_w.reshape(3, slots, HEAD_DIM, width).transpose(1, 0, 2, 3)
    qkv_w = qkv_w.reshape(slots, 3 * HEAD_DIM, width)
    last_qkv_w = last_w.reshape(3 * HEAD_DIM, width)
    bias_full = jnp.stack((b_qv[0], jnp.zeros_like(b_qv[0]), b_qv[1])).astype(jnp.float32)
    own_bias = lax.dynamic_slice_in_dim(bias_full, tensor_index * head_rows, head_rows, 1)
    own_bias = own_bias.reshape(3, slots, HEAD_DIM).transpose(1, 0, 2).reshape(slots, -1)
    last_bias = bias_full[:, whole_heads:].reshape(-1)

    half = unit_slab // 2
    quarter = half // chips
    unit_start = core_index * half + chip_index * quarter
    up_piece = lax.dynamic_slice_in_dim(w_up, unit_start, quarter, 1).T
    down_piece = lax.dynamic_slice_in_dim(w_down, unit_start, quarter, 0)
    bias_row = lax.dynamic_slice_in_dim(b_up, unit_start, quarter, 0)
    bias_row = jnp.pad(bias_row, (0, width - quarter))[None]
    out_rows = slab // chips if slab % chips == 0 else 0
    padded = -(-(out_rows + 1) // 8) * 8
    out_piece = lax.dynamic_slice_in_dim(w_out, chip_index * out_rows, out_rows, 0)
    filler = jnp.zeros((padded - out_rows - 1, width), low)
    pieces = [out_piece, bias_row, filler, up_piece, down_piece]
    pieces = jnp.concatenate(pieces, axis=0) + nothing(wide_one).astype(low)
    gathered = lax.all_gather(pieces, sharers, axis=0, tiled=True)
    gathered = gathered.reshape(tensor_size * chips, -1, width)
    up_bias = gathered[:, out_rows, :quarter].reshape(-1)
    if out_rows:
        full_out = gathered[:, :out_rows].reshape(width, width)
    else:
        full_out = lax.all_gather(w_out, "tensor", axis=0, tiled=True)
    half_up = gathered[:, padded : padded + quarter].reshape(-1, width)
    half_down = gathered[:, padded + quarter :].reshape(-1, width)
    wide_grad = jnp.concatenate((cotangent, other_core(cotangent)), axis=0)

    offsets = jnp.arange(tensor_size, dtype=jnp.int32)[:, None] * rows
    offsets = (offsets + jnp.arange(part, dtype=jnp.int32)[None]).reshape(-1)
    dp_starts = jnp.arange(dp_size, dtype=jnp.int32) * (tensor_size * rows)
    query_pos = dp_starts[:, None] + offsets[None] + member * part
    halves = jnp.arange(members, dtype=jnp.int32)
    if members == 2:
        halves = lax.rem(member + halves, 2)
    key_base = halves[:, None] * part + dp_starts[None]
    bases = [key_base[0], key_base[1]] if members == 2 else [key_base.reshape(-1)]
    plans = [attention_plan(query_pos, base, offsets, seq_ends) for base in bases]
    row_range = jnp.arange(rows, dtype=jnp.int32)
    steps_back = min(-(-REACH // tensor_size), dp_size - 1) + 1
    last_base = dp_index - jnp.arange(steps_back, dtype=jnp.int32)
    distance = tensor_index + tensor_size - jnp.arange(tensor_size, dtype=jnp.int32)
    last_base = last_base[None] * tensor_size + lax.rem(distance, tensor_size)[:, None]
    last_base = last_base.reshape(-1) * rows
    last_plan = attention_plan(
        (flat_index * rows + row_range)[None], last_base, row_range, seq_ends
    )

    qkv = jnp.einsum("cfd,gtd->cgft", qkv_w, wide_one, preferred_element_type=jnp.float32)
    qkv = (qkv + own_bias[:, None, :, None]).astype(low).reshape(dp_size, 3 * HEAD_DIM, lanes)
    qkv = lax.all_to_all(qkv, layer, split_axis=0, concat_axis=0, tiled=True)
    last_qkv = jnp.einsum("fd,td->ft", last_qkv_w, pre_one, preferred_element_type=jnp.float32)
    last_qkv = (last_qkv + last_bias[:, None]).astype(low)[None]
    own_pairs = qkv[:, HEAD_DIM:]
    last_pairs = last_qkv[:, HEAD_DIM:]
    last_pairs = [last_pairs] + [
        lax.ppermute(last_pairs, layer, line(dp_size, step)) for step in range(1, steps_back)
    ]
    last_blocks = gather_ring(jnp.concatenate(last_pairs, axis=0))
    sharing = [list(range(i, i + members)) for i in range(0, dp_size, members)]
    if members == 2:
        pairs = [own_pairs, other_core(own_pairs)]
    else:
        pairs = [lax.all_gather(own_pairs, layer, axis_index_groups=sharing, axis=0, tiled=True)]
    mixed, mixed_low, total = attend(qkv, pairs, plans, part, last_blocks)
    attended = lax.all_to_all(mixed_low, everywhere, split_axis=0, concat_axis=0, tiled=True)
    last_pairs = jnp.concatenate(last_blocks, axis=0)
    last_mixed, last_low, last_total = attend(
        after(last_qkv, total), [last_pairs], [last_plan], rows, ()
    )

    attended = attended.reshape(slots, members, tensor_size, HEAD_DIM, part)
    attended = attended.transpose(1, 2, 0, 3, 4).reshape(members, whole_heads, part)
    branch = jnp.einsum(
        "gkt,kd->gtd", attended, full_out[:whole_heads], preferred_element_type=jnp.float32
    ).reshape(rows, width)
    branch = branch + lax.dot_general(
        last_low[0], full_out[whole_heads:], contract_first, preferred_element_type=jnp.float32
    )
    stream_one = stream + branch + b_out.astype(jnp.float32)
    normed_two, inv_two, pre_two = norm_forward(stream_one, gain_two, shift_two)
    pre_two = pre_two.astype(low)
    wide_two = jnp.concatenate((pre_two, other_core(pre_two)), axis=0)
    hidden_pre = lax.dot_general(
        wide_two, half_up, contract_cols, preferred_element_type=jnp.float32
    ) + up_bias.astype(jnp.float32)
    gelu_out, gelu_pull = jax.vjp(
        lambda hidden_in: jax.nn.gelu(hidden_in, approximate=True), hidden_pre
    )
    activated = gelu_out.astype(low)
    grad_act = lax.dot_general(
        wide_grad, half_down, contract_cols, preferred_element_type=jnp.float32
    )
    grad_hidden = gelu_pull(grad_act)[0].astype(low)
    grad_up_part = jnp.sum(grad_hidden.astype(jnp.float32), axis=0)
    grad_two = cotangent.astype(jnp.float32)
    grad_down_bias = jnp.sum(grad_two, axis=0)
    grad_normed_two = jnp.dot(grad_hidden, half_up, preferred_element_type=jnp.float32)
    grad_normed_two = grad_normed_two[:rows] + other_core(
        grad_normed_two[rows:].astype(low)
    ).astype(jnp.float32)
    down_sum = jnp.dot(activated, half_down, preferred_element_type=jnp.float32)
    down_sum = down_sum[:rows] + other_core(down_sum[rows:].astype(low)).astype(jnp.float32)
    block_out = (stream_one + down_sum + b_down.astype(jnp.float32)).astype(low)
    grad_res_two, grad_gain_two, grad_shift_two = norm_backward(
        grad_normed_two, normed_two, inv_two, gain_two
    )
    grad_stream_one = grad_two + grad_res_two
    grad_branch = grad_stream_one.astype(low)
    grad_out_bias = jnp.sum(grad_branch.astype(jnp.float32), axis=0)

    branch_parts = grad_branch.reshape(members, part, width)
    grads = jnp.einsum(
        "kd,gtd->gkt", full_out[:whole_heads], branch_parts, preferred_element_type=jnp.float32
    )
    grads = grads.astype(low).reshape(members, tensor_size, slots, HEAD_DIM, part)
    grads = grads.transpose(2, 0, 1, 3, 4).reshape(devices, HEAD_DIM, part)
    grads = lax.all_to_all(grads, everywhere, split_axis=0, concat_axis=0, tiled=True)
    last_grads = lax.dot_general(
        full_out[whole_heads:], grad_branch, contract_cols, preferred_element_type=jnp.float32
    )
    last_grads = last_grads.astype(low)[None]
    last_query_grad, last_pair_grad = attend_back(
        last_qkv, last_pairs, last_plan, (last_grads, last_mixed, last_total), (), True, ()
    )
    column = width // dp_size
    grad_down = lax.dot_general(
        wide_grad, activated, contract_first, preferred_element_type=jnp.float32
    ).astype(low)
    grad_up = lax.dot_general(
        wide_two, grad_hidden, contract_first, preferred_element_type=jnp.float32
    ).astype(low)
    grad_out = jnp.einsum(
        "gtd,gkt->dk", branch_parts, attended, preferred_element_type=jnp.float32
    )
    last_out = lax.dot_general(
        grad_branch, last_low[0], (((0,), (1,)), ((), ())), preferred_element_type=jnp.float32
    )
    grad_out = jnp.concatenate((grad_out, last_out), axis=1).astype(low)
    low_bit, high_bit = chip_bits()
    if chips != 4:
        grad_down = lax.psum_scatter(grad_down, "chip", scatter_dimension=0, tiled=True)
        grad_up = lax.psum_scatter(grad_up, "chip", scatter_dimension=0, tiled=True)
        grad_out = lax.psum_scatter(grad_out, "chip", scatter_dimension=0, tiled=True)
    last_pair_grad = last_pair_grad.reshape(tensor_size, steps_back, 2 * HEAD_DIM, rows)
    last_arrived = [last_pair_grad[0]]
    for step in range(1, tensor_size):
        back = [(i, (i - step) % tensor_size) for i in range(tensor_size)]
        last_arrived.append(lax.ppermute(last_pair_grad[step], "tensor", back))
    known = (grads, mixed, total)
    if members == 2:
        query_state, pair_grad = attend_back(qkv, pairs[1], plans[1], known, (), False, ())
        other_grad = other_core(pair_grad)
        last_arrived = after(last_arrived, query_state)
        last_arrived = sum(block.astype(jnp.float32) for block in last_arrived)
        last_blocks = [
            lax.ppermute(last_arrived[step].astype(low), layer, line(dp_size, -step))
            for step in range(1, steps_back)
        ]
        if chips == 4:
            blocked = (2, 2, 2 * column, -1)
            grad_down = halve(grad_down.reshape(blocked), 0, flip(2), high_bit, query_state)
            grad_up = halve(grad_up.reshape(blocked), 1, flip(1), low_bit, query_state)
            grad_out = halve(grad_out.reshape(blocked), 1, flip(1), low_bit, query_state)
        query_grad, pair_grad = attend_back(
            qkv, pairs[0], plans[0], known, (query_state,), True, (grad_down, grad_up, grad_out)
        )
        if chips == 4:
            grad_down = halve(grad_down, 0, flip(1), low_bit, query_grad)
            grad_up = halve(grad_up, 0, flip(2), high_bit, query_grad)
            grad_out = halve(grad_out, 0, flip(2), high_bit, query_grad)
        last_sum = last_arrived[0]
        for block in after(last_blocks, query_grad):
            last_sum = last_sum + block.astype(jnp.float32)
        pair_sum = pair_grad.astype(jnp.float32) + other_grad.astype(jnp.float32)
    else:
        last_arrived = sum(block.astype(jnp.float32) for block in last_arrived)
        last_sum = last_arrived[0]
        for step in range(1, steps_back):
            arrived = lax.ppermute(last_arrived[step].astype(low), layer, line(dp_size, -step))
            last_sum = last_sum + arrived.astype(jnp.float32)
        query_grad, pair_grad = attend_back(qkv, pairs[0], plans[0], known, (), True, ())
        pair_grad = pair_grad.reshape(members, dp_size, 2 * HEAD_DIM, lanes)
        pair_grad = lax.all_to_all(pair_grad, layer, 0, 0, axis_index_groups=sharing, tiled=True)
        pair_sum = jnp.sum(pair_grad.astype(jnp.float32), axis=0)
    last_pair_grad = last_sum.astype(low)
    qkv_grad = jnp.concatenate((query_grad, pair_sum.astype(low)), axis=1)
    qkv_grad = lax.all_to_all(qkv_grad, layer, split_axis=0, concat_axis=0, tiled=True)
    qkv_grad = qkv_grad.reshape(slots, members, 3 * HEAD_DIM, lanes)
    last_qkv_grad = jnp.concatenate((last_query_grad[0], last_pair_grad), axis=0)

    units = jnp.stack((grad_up, grad_down)).reshape(2, 2 * column, tensor_size, half)
    units = units.transpose(2, 0, 1, 3)
    units = scatter_ring(units)
    zero = nothing(units)
    grad_normed_one = []
    for piece in range(members):
        product = jnp.einsum(
            "cfd,cft->dt", qkv_w, qkv_grad[:, piece], preferred_element_type=jnp.float32
        )
        product = (product + zero).astype(low).T.reshape(tensor_size, part, width)
        grad_normed_one.append(scatter_tensor(product))
    grad_normed_one = jnp.concatenate(grad_normed_one, axis=0)
    last_normed_one = lax.dot_general(
        last_qkv_grad, last_qkv_w, contract_first, preferred_element_type=jnp.float32
    )
    head = tensor_index * slots + lax.div(dp_index, members)
    own_sums = (jnp.sum(query_grad.astype(jnp.float32), axis=(0, 2)),)
    own_sums += (jnp.sum(pair_sum[:, HEAD_DIM:], axis=(0, 2)),)
    last_sums = jnp.sum(last_qkv_grad.astype(jnp.float32), axis=1).reshape(3, HEAD_DIM)
    qv_sum = jnp.zeros((2, HEADS, HEAD_DIM), jnp.float32).at[:, HEADS - 1].set(last_sums[::2])
    qv_sum = lax.dynamic_update_slice_in_dim(qv_sum, jnp.stack(own_sums)[:, None], head, 1)
    up_full = lax.dynamic_update_slice_in_dim(
        jnp.zeros((tensor_size, unit_slab), jnp.float32),
        grad_up_part.reshape(tensor_size, half),
        core_index * half,
        1,
    ).reshape(-1)
    early = jnp.concatenate(
        (grad_out_bias, grad_gain_two, grad_shift_two, grad_down_bias, up_full, qv_sum.reshape(-1))
    )
    early = butterfly(early)
    qv_sum = early[-2 * width :].reshape(2, width)
    early, up_sum = early[: 4 * width].reshape(4, width), early[4 * width : -2 * width]
    grad_normed_one = grad_normed_one + last_normed_one + nothing(early)
    grad_res_one, grad_gain_one, grad_shift_one = norm_backward(
        grad_normed_one, normed_one, inv_one, gain_one
    )
    grad_input = grad_stream_one + grad_res_one

    units = units.astype(low).reshape(2, 2, column, half)
    kept = pick(units, core_index, 1)
    arrived = other_core(pick(units, 1 - core_index, 1))
    units = (
        jnp.where(core_index == 0, kept, arrived),
        jnp.where(core_index == 0, arrived, kept),
    )
    units = jnp.concatenate(units, axis=2).astype(jnp.float32)
    grad_out = grad_out.reshape(2 * column, tensor_size, slab).transpose(1, 0, 2)
    grad_out = scatter_ring(grad_out).reshape(2, column, slab)
    sent = other_core(pick(grad_out, 1 - core_index, 0).astype(low))
    grad_out = (pick(grad_out, core_index, 0) + sent.astype(jnp.float32)).T

    own_qkv_grad = jnp.einsum(
        "gtd,cgft->dcf", wide_one, qkv_grad, preferred_element_type=jnp.float32
    )
    last_part = lax.dot_general(
        pre_one, last_qkv_grad, (((0,), (1,)), ((), ())), preferred_element_type=jnp.float32
    )
    grad_qkv = jnp.concatenate((own_qkv_grad.reshape(width, -1), last_part), axis=1).astype(low)
    if chips == 4:
        grad_qkv = grad_qkv.reshape(2, 2, 2, column, -1)
        sent = other_core(pick(grad_qkv, 1 - core_index, 2))
        kept = pick(grad_qkv, core_index, 2).astype(jnp.float32)
        grad_qkv = (kept + sent.astype(jnp.float32)).astype(low)
        grad_qkv = halve(grad_qkv, 1, flip(1), low_bit, None)
        grad_qkv = halve(grad_qkv, 0, flip(2), high_bit, None)
    else:
        grad_qkv = lax.psum_scatter(grad_qkv, layer, scatter_dimension=0, tiled=True)
    own_qkv_grad = grad_qkv[:, : 3 * head_rows].T.reshape(slots, 3, HEAD_DIM, column)
    own_qkv_grad = own_qkv_grad.transpose(1, 0, 2, 3).reshape(3, head_rows, column)
    last_part = grad_qkv[:, 3 * head_rows :].T.reshape(3, HEAD_DIM, column)
    last_sum = last_part.astype(jnp.float32)
    for source in range(tensor_size - 1):
        arrived = lax.ppermute(last_part, "tensor", [(source, tensor_size - 1)])
        last_sum = last_sum + arrived.astype(jnp.float32)
    grad_qkv = slab_rows(own_qkv_grad, last_sum.astype(low), slab, tensor_size, tensor_index)
    grad_qkv = grad_qkv.astype(jnp.float32)

    late = small_sum(jnp.stack((grad_gain_one, grad_shift_one)))
    grad_up_bias = lax.dynamic_slice_in_dim(up_sum, tensor_index * unit_slab, unit_slab, 0)
    return (
        block_out,
        grad_input,
        late[0],
        late[1],
        grad_qkv,
        qv_sum,
        grad_out,
        early[0],
        early[1],
        early[2],
        units[0],
        grad_up_bias,
        units[1].T,
        early[3],
    )


def solution(mesh):
    chips, tensor = mesh.shape["dp"] // 2, mesh.shape["tensor"]
    cores = jax.sharding.Mesh(mesh.devices.reshape(chips, 2, tensor), everywhere)
    in_specs = (
        P(everywhere, None),
        P(),
        P(),
        P(None, "tensor", None),
        P(),
        P("tensor", None),
        P(),
        P(),
        P(),
        P(None, "tensor"),
        P("tensor"),
        P("tensor", None),
        P(),
        P(),
        P(everywhere, None),
    )
    out_specs = (
        P(everywhere, None),
        P(everywhere, None),
        P(),
        P(),
        P(None, "tensor", layer),
        P(),
        P("tensor", layer),
        P(),
        P(),
        P(),
        P(layer, "tensor"),
        P("tensor"),
        P("tensor", layer),
        P(),
    )
    return jax.shard_map(local, mesh=cores, in_specs=in_specs, out_specs=out_specs, check_vma=False)
```

```python
import jax
import jax.numpy as jnp
from jax import lax
from jax.experimental import pallas as pl
from jax.experimental.pallas import tpu as pltpu
from jax.sharding import PartitionSpec as P

HEADS = 17
HEAD_DIM = 64
REACH = 11

norm_eps = 1e-05
score_scale = 0.125
masked_score = -1e30
everywhere = ("chip", "core", "tensor")
layer = ("chip", "core")
sharers = ("tensor", "chip")


def line(count, steps):
    first, last = (max(0, -steps), min(count, count - steps))
    return [(source, source + steps) for source in range(first, last)]


def gather_tensor(rows, axis):
    count = lax.axis_size("tensor")
    index = lax.axis_index("tensor")
    up, down = [rows], [rows]
    for _ in range(count - 1):
        up.append(lax.ppermute(up[-1], "tensor", line(count, 1)))
        down.append(lax.ppermute(down[-1], "tensor", line(count, -1)))
    shape = rows.shape[:axis] + (count,) + rows.shape[axis:]
    gathered = lax.dynamic_update_index_in_dim(jnp.zeros(shape, rows.dtype), rows, index, axis)
    for steps in range(1, count):
        block = jnp.where(index >= steps, up[steps], down[count - steps])
        gathered = lax.dynamic_update_index_in_dim(
            gathered, block, lax.rem(index - steps + count, count), axis
        )
    return gathered


def scatter_tensor(partial_sum):
    arrived = lax.all_to_all(partial_sum, "tensor", split_axis=0, concat_axis=0, tiled=True)
    return jnp.sum(arrived.astype(jnp.float32), axis=0)


def after(value, token):
    return lax.optimization_barrier((value, token))[0]


def other_core(value):
    return lax.ppermute(value, "core", [(0, 1), (1, 0)])


def small_sum(value):
    count = lax.axis_size(everywhere)
    copies = jnp.broadcast_to(value[None], (count,) + value.shape)
    arrived = lax.all_to_all(copies, everywhere, split_axis=0, concat_axis=0, tiled=True)
    return jnp.sum(arrived, axis=0)


def nothing(value):
    return jnp.minimum(jnp.abs(value[(0,) * value.ndim].astype(jnp.float32)), 0.0)


def pick(value, index, axis):
    return lax.dynamic_index_in_dim(value, index, axis, keepdims=False)


def halve(value, axis, neighbour, index, token):
    sent = lax.ppermute(pick(value, 1 - index, axis), "chip", neighbour)
    if token is not None:
        sent = after(sent, token)
    kept = pick(value, index, axis).astype(jnp.float32) + sent.astype(jnp.float32)
    return kept.astype(jnp.bfloat16)


def flip(bit):
    return [(i, i ^ bit) for i in range(4)]


def chip_bits():
    index = lax.axis_index("chip")
    return lax.rem(index, 2), lax.div(index, 2)


def scatter_ring(both):
    tensor_size, index = lax.axis_size("tensor"), lax.axis_index("tensor")
    total = pick(both, index, 0).astype(jnp.float32)
    for steps in range(1, tensor_size):
        ring = [(i, (i + steps) % tensor_size) for i in range(tensor_size)]
        arrived = lax.ppermute(pick(both, lax.rem(index + steps, tensor_size), 0), "tensor", ring)
        total = total + arrived.astype(jnp.float32)
    return total


def sum_offsets(blocks):
    tensor_size, index = lax.axis_size("tensor"), lax.axis_index("tensor")
    total = 0.0
    for steps, block in enumerate(blocks):
        block = block.astype(jnp.float32)
        near, far = (jnp.pad(block, (ends, (0, 0), (0, 0))) for ends in ((0, 1), (1, 0)))
        total = total + jnp.where(index + steps >= tensor_size, far, near)
    return total


def gather_ring(block):
    tensor_size = lax.axis_size("tensor")
    index, needed = lax.axis_index("tensor"), block.shape[0] - 1
    blocks = [block[:needed]]
    for steps in range(1, tensor_size):
        ring = [(i, (i + steps) % tensor_size) for i in range(tensor_size)]
        first = (index + steps >= tensor_size).astype(jnp.int32)
        sent = lax.dynamic_slice_in_dim(block, first, needed, 0)
        blocks.append(lax.ppermute(sent, "tensor", ring))
    return blocks


def butterfly(value):
    for axis in ("core", "chip", "tensor"):
        count = lax.axis_size(axis)
        step = 1
        while step < count:
            value = value + lax.ppermute(value, axis, [(i, i ^ step) for i in range(count)])
            step *= 2
    return value


def norm_forward(values, gain_vec, bias_vec):
    mean_row = jnp.mean(values, axis=1, keepdims=True)
    centered = values - mean_row
    variance = jnp.mean(centered * centered, axis=1, keepdims=True)
    inv_std = lax.rsqrt(variance + norm_eps)
    normed = centered * inv_std
    return (normed, inv_std, normed * gain_vec + bias_vec)


def norm_backward(grad_normed, normed, inv_std, gain_vec):
    scaled = grad_normed * gain_vec
    plain_mean = jnp.mean(scaled, axis=1, keepdims=True)
    cross_mean = jnp.mean(scaled * normed, axis=1, keepdims=True)
    grad_values = inv_std * (scaled - plain_mean - normed * cross_mean)
    return (grad_values, jnp.sum(grad_normed * normed, axis=0), jnp.sum(grad_normed, axis=0))


def tile_of(width):
    return 384 if width % 384 == 0 else width


def attention_plan(query_pos, key_base, key_offsets, seq_ends):
    width = query_pos.shape[1]
    key_width = key_offsets.shape[0]
    tile, key_tile = tile_of(width), tile_of(key_width)
    starts = jnp.max(
        jnp.where(seq_ends[None, None, :] <= query_pos[:, :, None], seq_ends[None, None, :], 0),
        axis=2,
    )
    rows = jnp.stack((query_pos, starts), axis=1)
    tiles = query_pos.reshape(-1, tile)
    first, last = tiles[:, 0], tiles[:, tile - 1]
    last_start = starts.reshape(-1, tile)[:, tile - 1]
    offset_tiles = key_offsets.reshape(-1, key_tile)
    key_min = (key_base[:, None] + offset_tiles[None, :, 0]).reshape(-1)
    key_max = (key_base[:, None] + offset_tiles[None, :, key_tile - 1]).reshape(-1)
    key_end = jnp.min(
        jnp.where(seq_ends[None, :] > key_max[:, None], seq_ends[None, :], seq_ends[-1]), axis=1
    )
    low = jnp.sum((last[None, :] < key_min[:, None]).astype(jnp.int32), axis=1)
    high = jnp.sum((first[None, :] < key_end[:, None]).astype(jnp.int32), axis=1)
    bases = jnp.repeat(key_base, key_width // key_tile)
    plan = jnp.concatenate((low, high, bases, key_min, key_max, first, last_start))
    return (plan.astype(jnp.int32), rows.astype(jnp.int32), key_offsets[:, None].astype(jnp.int32))


def key_allowed(column_ref, rows_ref, step, per_key, key_tile, base, group, lanes):
    offset = pl.multiple_of(lax.rem(step, per_key) * key_tile, key_tile)
    key_pos = column_ref[pl.ds(offset, key_tile), :] + base
    query_pos = rows_ref[group, 0:1, lanes]
    query_start = rows_ref[group, 1:2, lanes]
    return (key_pos <= query_pos) & (key_pos >= query_start)


def forward_kernel(dims, ends, plan_ref, query_ref, pair_ref, rows_ref, column_ref, *more):
    first, final = ends
    state, more = ((), more) if first else (more[:3], more[3:])
    outs, (acc, top, tot) = more[:3], more[3:]
    blocks, groups, per_query, per_key, tile, key_tile, part = dims
    count = groups * per_query
    step = pl.program_id(0)

    @pl.when(step == 0)
    def _():
        if first:
            acc[...] = jnp.zeros_like(acc)
            top[...] = jnp.full(top.shape, masked_score, jnp.float32)
            tot[...] = jnp.zeros_like(tot)
        else:
            for held, given in zip((acc, top, tot), state):
                held[...] = given[...]

    keys = jnp.transpose(pair_ref[0, :HEAD_DIM, :].astype(jnp.float32)).astype(jnp.bfloat16)
    values_t = pair_ref[0, HEAD_DIM:, :]
    base, key_min, key_max = (plan_ref[kind * blocks + step] for kind in (2, 3, 4))

    def one_tile(index, _):
        group = lax.div(index, per_query)
        lanes = pl.ds(pl.multiple_of(lax.rem(index, per_query) * tile, tile), tile)
        queries_t = query_ref[group, :HEAD_DIM, lanes] * jnp.bfloat16(score_scale)
        inside = (key_max <= plan_ref[5 * blocks + index]) & (
            key_min >= plan_ref[5 * blocks + count + index]
        )

        def update(masked):
            scores = jnp.dot(keys, queries_t, preferred_element_type=jnp.float32)
            if masked:
                allowed = key_allowed(
                    column_ref, rows_ref, step, per_key, key_tile, base, group, lanes
                )
                scores = jnp.where(allowed, scores, masked_score)
            old_top = top[index]
            new_top = jnp.maximum(old_top, jnp.max(scores, axis=0, keepdims=True))
            weights = jnp.exp(scores - new_top)
            shrink = jnp.exp(old_top - new_top)
            top[index] = new_top
            tot[index] = tot[index] * shrink + jnp.sum(weights, axis=0, keepdims=True)
            acc[index] = acc[index] * shrink + jnp.dot(
                values_t, weights.astype(jnp.bfloat16), preferred_element_type=jnp.float32
            )

        pl.when(inside)(lambda: update(False))
        pl.when(jnp.logical_not(inside))(lambda: update(True))
        return 0

    lax.fori_loop(plan_ref[step], plan_ref[blocks + step], one_tile, 0)

    @pl.when(step == blocks - 1)
    def _():
        if not final:
            for held, given in zip(outs, (acc, top, tot)):
                held[...] = given[...]
            return
        out_ref, low_ref, total_ref = outs

        def finish(index, _):
            group = lax.div(index, per_query)
            lanes = pl.ds(pl.multiple_of(lax.rem(index, per_query) * tile, tile), tile)
            result = acc[index] / tot[index]
            out_ref[group, :, lanes] = result
            for piece in range(tile // part):
                low_ref[index * (tile // part) + piece] = result[
                    :, piece * part : (piece + 1) * part
                ].astype(jnp.bfloat16)
            total_ref[index] = top[index] + jnp.log(tot[index])
            return 0

        lax.fori_loop(0, count, finish, 0)


def backward_kernel(
    dims,
    ends,
    plan_ref,
    query_ref,
    pair_ref,
    rows_ref,
    column_ref,
    grad_ref,
    out_ref,
    total_ref,
    *more,
):
    first, final = ends
    state, more = ((), more) if first else (more[:1], more[1:])
    query_grad_ref, pair_grad_ref, acc, inner, grad_cols, query_rows, grad_rows = more[:7]
    key_acc, value_acc = more[7:]
    blocks, groups, per_query, per_key, tile, key_tile, part = dims
    count = groups * per_query
    step = pl.program_id(0)

    @pl.when(step == 0)
    def _():
        acc[...] = jnp.zeros_like(acc) if first else state[0][...]

        def prepare(index, _):
            group = lax.div(index, per_query)
            lanes = pl.ds(pl.multiple_of(lax.rem(index, per_query) * tile, tile), tile)
            for piece in range(tile // part):
                grad_cols[index, :, piece * part : (piece + 1) * part] = grad_ref[
                    index * (tile // part) + piece
                ]
            grads = grad_cols[index].astype(jnp.float32)
            inner[index] = jnp.sum(grads * out_ref[group, :, lanes], axis=0, keepdims=True)
            grad_rows[index] = jnp.transpose(grads).astype(jnp.bfloat16)
            scaled = query_ref[group, :HEAD_DIM, lanes].astype(jnp.float32) * score_scale
            query_rows[index] = jnp.transpose(scaled).astype(jnp.bfloat16)
            return 0

        lax.fori_loop(0, count, prepare, 0)

    keys_t = pair_ref[0, :HEAD_DIM, :]
    keys = jnp.transpose(keys_t.astype(jnp.float32)).astype(jnp.bfloat16)
    values = jnp.transpose(pair_ref[0, HEAD_DIM:, :].astype(jnp.float32)).astype(jnp.bfloat16)
    base, key_min, key_max = (plan_ref[kind * blocks + step] for kind in (2, 3, 4))
    key_acc[...] = jnp.zeros_like(key_acc)
    value_acc[...] = jnp.zeros_like(value_acc)

    def one_tile(index, _):
        group = lax.div(index, per_query)
        lanes = pl.ds(pl.multiple_of(lax.rem(index, per_query) * tile, tile), tile)
        queries_t = query_ref[group, :HEAD_DIM, lanes] * jnp.bfloat16(score_scale)
        grads_t = grad_cols[index]
        inside = (key_max <= plan_ref[5 * blocks + index]) & (
            key_min >= plan_ref[5 * blocks + count + index]
        )

        def update(masked):
            scores = jnp.dot(keys, queries_t, preferred_element_type=jnp.float32)
            weights = jnp.exp(scores - total_ref[index])
            if masked:
                allowed = key_allowed(
                    column_ref, rows_ref, step, per_key, key_tile, base, group, lanes
                )
                weights = jnp.where(allowed, weights, 0.0)
            grad_weights = jnp.dot(values, grads_t, preferred_element_type=jnp.float32)
            grad_scores = (weights * (grad_weights - inner[index])).astype(jnp.bfloat16)
            value_acc[...] += jnp.dot(
                weights.astype(jnp.bfloat16), grad_rows[index], preferred_element_type=jnp.float32
            )
            key_acc[...] += jnp.dot(
                grad_scores, query_rows[index], preferred_element_type=jnp.float32
            )
            acc[index] += jnp.dot(keys_t, grad_scores, preferred_element_type=jnp.float32)

        pl.when(inside)(lambda: update(False))
        pl.when(jnp.logical_not(inside))(lambda: update(True))
        return 0

    lax.fori_loop(plan_ref[step], plan_ref[blocks + step], one_tile, 0)
    pair_grad_ref[0, :HEAD_DIM, :] = jnp.transpose(key_acc[...]).astype(jnp.bfloat16)
    pair_grad_ref[0, HEAD_DIM:, :] = jnp.transpose(value_acc[...]).astype(jnp.bfloat16)

    @pl.when(step == blocks - 1)
    def _():
        if not final:
            query_grad_ref[...] = acc[...]
            return

        def finish(index, _):
            group = lax.div(index, per_query)
            lanes = pl.ds(pl.multiple_of(lax.rem(index, per_query) * tile, tile), tile)
            query_grad_ref[group, :, lanes] = (acc[index] * score_scale).astype(jnp.bfloat16)
            return 0

        lax.fori_loop(0, count, finish, 0)


def attention_call(kernel, ends, queries, pairs, plan, more, part, outs, scratch, flops, tokens):
    numbers, rows, column = plan
    groups, _, width = queries.shape
    key_groups, _, key_width = pairs.shape
    tile, key_tile = tile_of(width), tile_of(key_width)
    per_query, per_key = width // tile, key_width // key_tile
    blocks = key_groups * per_key
    count = groups * per_query

    def whole(array):
        return pl.BlockSpec(array.shape, lambda step, plan_ref: (0,) * array.ndim)

    pair_spec = pl.BlockSpec(
        (1, 2 * HEAD_DIM, key_tile),
        lambda step, plan_ref: (lax.div(step, per_key), 0, lax.rem(step, per_key)),
    )
    out_shapes, out_specs = [], []
    for kind in outs:
        if kind == "pairs":
            out_shapes.append(jax.ShapeDtypeStruct(pairs.shape, jnp.bfloat16))
            out_specs.append(pair_spec)
        else:
            shape = {
                "row": (count, 1, tile),
                "acc": (count, HEAD_DIM, tile),
                "low": (groups * width // part, HEAD_DIM, part),
            }.get(kind, (groups, HEAD_DIM, width))
            dtype = jnp.bfloat16 if kind in ("grads", "low") else jnp.float32
            out_shapes.append(jax.ShapeDtypeStruct(shape, dtype))
            out_specs.append(whole(out_shapes[-1]))
    sizes = {
        "acc": pltpu.VMEM((count, HEAD_DIM, tile), jnp.float32),
        "row": pltpu.VMEM((count, 1, tile), jnp.float32),
        "cols": pltpu.VMEM((count, HEAD_DIM, tile), jnp.bfloat16),
        "rows": pltpu.VMEM((count, tile, HEAD_DIM), jnp.bfloat16),
        "keys": pltpu.VMEM((key_tile, HEAD_DIM), jnp.float32),
    }
    position = 5 + len(more)

    def body(*refs):
        kernel(dims, ends, *refs[:position], *refs[position + len(tokens) :])

    dims = (blocks, groups, per_query, per_key, tile, key_tile, part)
    pairs_near = groups * width * min(key_groups * key_width, 2304)
    return pl.pallas_call(
        body,
        out_shape=out_shapes,
        grid_spec=pltpu.PrefetchScalarGridSpec(
            num_scalar_prefetch=1,
            grid=(blocks,),
            in_specs=[whole(queries), pair_spec, whole(rows), whole(column)]
            + [whole(array) for array in more]
            + [pl.BlockSpec(memory_space=pl.ANY)] * len(tokens),
            out_specs=out_specs,
            scratch_shapes=[sizes[name] for name in scratch],
        ),
        compiler_params=pltpu.CompilerParams(
            dimension_semantics=("arbitrary",), vmem_limit_bytes=56 * 2**20
        ),
        cost_estimate=pl.CostEstimate(
            flops=flops * pairs_near * HEAD_DIM,
            bytes_accessed=4 * queries.size + 4 * pairs.size,
            transcendentals=pairs_near,
        ),
    )(numbers, queries, pairs, rows, column, *more, *tokens)


def attend(queries, pairs, plans, part, tokens):
    state = ()
    for index, (keys, plan) in enumerate(zip(pairs, plans)):
        ends = (index == 0, index == len(pairs) - 1)
        if index == 1:
            keys = after(keys, state)
        state = attention_call(
            forward_kernel,
            ends,
            queries,
            keys,
            plan,
            tuple(state),
            part,
            ("out", "low", "row") if ends[1] else ("acc", "row", "row"),
            ("acc", "row", "row"),
            16,
            tuple(tokens) if ends[1] else (),
        )
    return state


def attend_back(queries, keys, plan, known, state, final, tokens):
    return attention_call(
        backward_kernel,
        (not state, final),
        queries,
        keys,
        plan,
        known + state,
        known[0].shape[2],
        ("grads" if final else "acc", "pairs"),
        ("acc", "row", "cols", "rows", "rows", "keys", "keys"),
        40,
        tokens,
    )


def aligned_weights(stacked, tensor_size, tensor_index, head_rows):
    slab = stacked.shape[1]
    extra = slab - head_rows
    most = (tensor_size - 1) * extra
    before = lax.ppermute(stacked[:, slab - most :], "tensor", line(tensor_size, 1))
    joined = jnp.concatenate((before, stacked), axis=1)
    own = lax.dynamic_slice_in_dim(joined, most - extra * tensor_index, head_rows, 1)
    return own


def last_weights(stacked, tensor_size, tensor_index):
    final = stacked[:, stacked.shape[1] - HEAD_DIM :]
    last = jnp.where(tensor_index == tensor_size - 1, final, jnp.zeros_like(final))
    for target in range(tensor_size - 1):
        last = last + lax.ppermute(final, "tensor", [(tensor_size - 1, target)])
    return last


def slab_rows(own, last, slab, tensor_size, tensor_index):
    extra = slab - own.shape[1]
    most = (tensor_size - 1) * extra
    following = lax.ppermute(own[:, :most], "tensor", line(tensor_size, -1))
    following = jnp.pad(following, ((0, 0), (0, HEAD_DIM - most), (0, 0)))
    following = jnp.where(tensor_index == tensor_size - 1, last, following)
    joined = jnp.concatenate((own, following), axis=1)
    return lax.dynamic_slice_in_dim(joined, extra * tensor_index, slab, 1)


def local(
    tokens_in,
    ln1_gain,
    ln1_bias,
    w_qkv,
    b_qv,
    w_out,
    b_out,
    ln2_gain,
    ln2_bias,
    w_up,
    b_up,
    w_down,
    b_down,
    seq_lengths,
    cotangent,
):
    tensor_size = lax.axis_size("tensor")
    tensor_index = lax.axis_index("tensor")
    chips = lax.axis_size("chip")
    chip_index = lax.axis_index("chip")
    core_index = lax.axis_index("core")
    dp_size = lax.axis_size(layer)
    dp_index = lax.axis_index(layer)
    flat_index = lax.axis_index(everywhere)
    devices = dp_size * tensor_size
    rows, width = tokens_in.shape
    slab = w_qkv.shape[1]
    unit_slab = w_up.shape[1]
    slots = (HEADS - 1) // tensor_size
    members = dp_size // slots
    member = lax.rem(dp_index, members)
    part = rows // members
    lanes = tensor_size * part
    head_rows = slots * HEAD_DIM
    whole_heads = width - HEAD_DIM
    low = jnp.bfloat16
    seq_ends = jnp.cumsum(seq_lengths)
    gain_one = ln1_gain.astype(jnp.float32)
    shift_one = ln1_bias.astype(jnp.float32)
    gain_two = ln2_gain.astype(jnp.float32)
    shift_two = ln2_bias.astype(jnp.float32)
    contract_first = (((0,), (0,)), ((), ()))
    contract_cols = (((1,), (1,)), ((), ()))

    stream = tokens_in.astype(jnp.float32)
    normed_one, inv_one, pre_one = norm_forward(stream, gain_one, shift_one)
    pre_one = pre_one.astype(low)
    wide_one = gather_tensor(pre_one.reshape(members, part, width), 1)
    wide_one = wide_one.reshape(members, lanes, width)
    own_w = aligned_weights(w_qkv, tensor_size, tensor_index, head_rows)
    last_w = last_weights(w_qkv, tensor_size, tensor_index)
    qkv_w = own_w.reshape(3, slots, HEAD_DIM, width).transpose(1, 0, 2, 3)
    qkv_w = qkv_w.reshape(slots, 3 * HEAD_DIM, width)
    last_qkv_w = last_w.reshape(3 * HEAD_DIM, width)
    bias_full = jnp.stack((b_qv[0], jnp.zeros_like(b_qv[0]), b_qv[1])).astype(jnp.float32)
    own_bias = lax.dynamic_slice_in_dim(bias_full, tensor_index * head_rows, head_rows, 1)
    own_bias = own_bias.reshape(3, slots, HEAD_DIM).transpose(1, 0, 2).reshape(slots, -1)
    last_bias = bias_full[:, whole_heads:].reshape(-1)

    half = unit_slab // 2
    quarter = half // chips
    unit_start = core_index * half + chip_index * quarter
    up_piece = lax.dynamic_slice_in_dim(w_up, unit_start, quarter, 1).T
    down_piece = lax.dynamic_slice_in_dim(w_down, unit_start, quarter, 0)
    bias_row = lax.dynamic_slice_in_dim(b_up, unit_start, quarter, 0)
    bias_row = jnp.pad(bias_row, (0, width - quarter))[None]
    out_rows = slab // chips if slab % chips == 0 else 0
    padded = -(-(out_rows + 1) // 8) * 8
    out_piece = lax.dynamic_slice_in_dim(w_out, chip_index * out_rows, out_rows, 0)
    filler = jnp.zeros((padded - out_rows - 1, width), low)
    pieces = [out_piece, bias_row, filler, up_piece, down_piece]
    pieces = jnp.concatenate(pieces, axis=0) + nothing(wide_one).astype(low)
    gathered = lax.all_gather(pieces, sharers, axis=0, tiled=True)
    gathered = gathered.reshape(tensor_size * chips, -1, width)
    up_bias = gathered[:, out_rows, :quarter].reshape(-1)
    if out_rows:
        full_out = gathered[:, :out_rows].reshape(width, width)
    else:
        full_out = lax.all_gather(w_out, "tensor", axis=0, tiled=True)
    half_up = gathered[:, padded : padded + quarter].reshape(-1, width)
    half_down = gathered[:, padded + quarter :].reshape(-1, width)
    wide_grad = jnp.concatenate((cotangent, other_core(cotangent)), axis=0)

    offsets = jnp.arange(tensor_size, dtype=jnp.int32)[:, None] * rows
    offsets = (offsets + jnp.arange(part, dtype=jnp.int32)[None]).reshape(-1)
    dp_starts = jnp.arange(dp_size, dtype=jnp.int32) * (tensor_size * rows)
    query_pos = dp_starts[:, None] + offsets[None] + member * part
    halves = jnp.arange(members, dtype=jnp.int32)
    if members == 2:
        halves = lax.rem(member + halves, 2)
    key_base = halves[:, None] * part + dp_starts[None]
    bases = [key_base[0], key_base[1]] if members == 2 else [key_base.reshape(-1)]
    plans = [attention_plan(query_pos, base, offsets, seq_ends) for base in bases]
    row_range = jnp.arange(rows, dtype=jnp.int32)
    steps_back = min(-(-REACH // tensor_size), dp_size - 1) + 1
    distance = jnp.arange(tensor_size, dtype=jnp.int32)
    wrapped = (distance > tensor_index).astype(jnp.int32)
    source = tensor_index - distance + wrapped * tensor_size
    last_base = dp_index - wrapped[:, None] - jnp.arange(steps_back - 1, dtype=jnp.int32)[None]
    last_base = (last_base * tensor_size + source[:, None]).reshape(-1) * rows
    last_plan = attention_plan(
        (flat_index * rows + row_range)[None], last_base, row_range, seq_ends
    )

    qkv = jnp.einsum("cfd,gtd->cgft", qkv_w, wide_one, preferred_element_type=jnp.float32)
    qkv = (qkv + own_bias[:, None, :, None]).astype(low).reshape(dp_size, 3 * HEAD_DIM, lanes)
    qkv = lax.all_to_all(qkv, layer, split_axis=0, concat_axis=0, tiled=True)
    last_qkv = jnp.einsum("fd,td->ft", last_qkv_w, pre_one, preferred_element_type=jnp.float32)
    last_qkv = (last_qkv + last_bias[:, None]).astype(low)[None]
    own_pairs = qkv[:, HEAD_DIM:]
    last_pairs = last_qkv[:, HEAD_DIM:]
    last_pairs = [last_pairs] + [
        lax.ppermute(last_pairs, layer, line(dp_size, step)) for step in range(1, steps_back)
    ]
    last_blocks = gather_ring(jnp.concatenate(last_pairs, axis=0))
    sharing = [list(range(i, i + members)) for i in range(0, dp_size, members)]
    if members == 2:
        pairs = [own_pairs, other_core(own_pairs)]
    else:
        pairs = [lax.all_gather(own_pairs, layer, axis_index_groups=sharing, axis=0, tiled=True)]
    mixed, mixed_low, total = attend(qkv, pairs, plans, part, last_blocks)
    attended = lax.all_to_all(mixed_low, everywhere, split_axis=0, concat_axis=0, tiled=True)
    last_pairs = jnp.concatenate(last_blocks, axis=0)
    last_mixed, last_low, last_total = attend(
        after(last_qkv, total), [last_pairs], [last_plan], rows, ()
    )

    attended = attended.reshape(slots, members, tensor_size, HEAD_DIM, part)
    attended = attended.transpose(1, 2, 0, 3, 4).reshape(members, whole_heads, part)
    branch = jnp.einsum(
        "gkt,kd->gtd", attended, full_out[:whole_heads], preferred_element_type=jnp.float32
    ).reshape(rows, width)
    branch = branch + lax.dot_general(
        last_low[0], full_out[whole_heads:], contract_first, preferred_element_type=jnp.float32
    )
    stream_one = stream + branch + b_out.astype(jnp.float32)
    normed_two, inv_two, pre_two = norm_forward(stream_one, gain_two, shift_two)
    pre_two = pre_two.astype(low)
    wide_two = jnp.concatenate((pre_two, other_core(pre_two)), axis=0)
    hidden_pre = lax.dot_general(
        wide_two, half_up, contract_cols, preferred_element_type=jnp.float32
    ) + up_bias.astype(jnp.float32)
    gelu_out, gelu_pull = jax.vjp(
        lambda hidden_in: jax.nn.gelu(hidden_in, approximate=True), hidden_pre
    )
    activated = gelu_out.astype(low)
    grad_act = lax.dot_general(
        wide_grad, half_down, contract_cols, preferred_element_type=jnp.float32
    )
    grad_hidden = gelu_pull(grad_act)[0].astype(low)
    grad_up_part = jnp.sum(grad_hidden.astype(jnp.float32), axis=0)
    grad_two = cotangent.astype(jnp.float32)
    grad_down_bias = jnp.sum(grad_two, axis=0)
    grad_normed_two = jnp.dot(grad_hidden, half_up, preferred_element_type=jnp.float32)
    grad_normed_two = grad_normed_two[:rows] + other_core(
        grad_normed_two[rows:].astype(low)
    ).astype(jnp.float32)
    down_sum = jnp.dot(activated, half_down, preferred_element_type=jnp.float32)
    down_sum = down_sum[:rows] + other_core(down_sum[rows:].astype(low)).astype(jnp.float32)
    block_out = (stream_one + down_sum + b_down.astype(jnp.float32)).astype(low)
    grad_res_two, grad_gain_two, grad_shift_two = norm_backward(
        grad_normed_two, normed_two, inv_two, gain_two
    )
    grad_stream_one = grad_two + grad_res_two
    grad_branch = grad_stream_one.astype(low)
    grad_out_bias = jnp.sum(grad_branch.astype(jnp.float32), axis=0)

    branch_parts = grad_branch.reshape(members, part, width)
    grads = jnp.einsum(
        "kd,gtd->gkt", full_out[:whole_heads], branch_parts, preferred_element_type=jnp.float32
    )
    grads = grads.astype(low).reshape(members, tensor_size, slots, HEAD_DIM, part)
    grads = grads.transpose(2, 0, 1, 3, 4).reshape(devices, HEAD_DIM, part)
    grads = lax.all_to_all(grads, everywhere, split_axis=0, concat_axis=0, tiled=True)
    last_grads = lax.dot_general(
        full_out[whole_heads:], grad_branch, contract_cols, preferred_element_type=jnp.float32
    )
    last_grads = last_grads.astype(low)[None]
    last_query_grad, last_pair_grad = attend_back(
        last_qkv, last_pairs, last_plan, (last_grads, last_mixed, last_total), (), True, ()
    )
    column = width // dp_size
    grad_down = lax.dot_general(
        wide_grad, activated, contract_first, preferred_element_type=jnp.float32
    ).astype(low)
    grad_up = lax.dot_general(
        wide_two, grad_hidden, contract_first, preferred_element_type=jnp.float32
    ).astype(low)
    grad_out = jnp.einsum(
        "gtd,gkt->dk", branch_parts, attended, preferred_element_type=jnp.float32
    )
    last_out = lax.dot_general(
        grad_branch, last_low[0], (((0,), (1,)), ((), ())), preferred_element_type=jnp.float32
    )
    grad_out = jnp.concatenate((grad_out, last_out), axis=1).astype(low)
    low_bit, high_bit = chip_bits()
    if chips != 4:
        grad_down = lax.psum_scatter(grad_down, "chip", scatter_dimension=0, tiled=True)
        grad_up = lax.psum_scatter(grad_up, "chip", scatter_dimension=0, tiled=True)
        grad_out = lax.psum_scatter(grad_out, "chip", scatter_dimension=0, tiled=True)
    last_pair_grad = last_pair_grad.reshape(tensor_size, steps_back - 1, 2 * HEAD_DIM, rows)
    last_arrived = [last_pair_grad[0]]
    for step in range(1, tensor_size):
        back = [(i, (i - step) % tensor_size) for i in range(tensor_size)]
        last_arrived.append(lax.ppermute(last_pair_grad[step], "tensor", back))
    known = (grads, mixed, total)
    if members == 2:
        query_state, pair_grad = attend_back(qkv, pairs[1], plans[1], known, (), False, ())
        other_grad = other_core(pair_grad)
        last_arrived = after(last_arrived, query_state)
        last_arrived = sum_offsets(last_arrived)
        last_blocks = [
            lax.ppermute(last_arrived[step].astype(low), layer, line(dp_size, -step))
            for step in range(1, steps_back)
        ]
        if chips == 4:
            blocked = (2, 2, 2 * column, -1)
            grad_down = halve(grad_down.reshape(blocked), 0, flip(2), high_bit, query_state)
            grad_up = halve(grad_up.reshape(blocked), 1, flip(1), low_bit, query_state)
            grad_out = halve(grad_out.reshape(blocked), 1, flip(1), low_bit, query_state)
        query_grad, pair_grad = attend_back(
            qkv, pairs[0], plans[0], known, (query_state,), True, (grad_down, grad_up, grad_out)
        )
        if chips == 4:
            grad_down = halve(grad_down, 0, flip(1), low_bit, query_grad)
            grad_up = halve(grad_up, 0, flip(2), high_bit, query_grad)
            grad_out = halve(grad_out, 0, flip(2), high_bit, query_grad)
        last_sum = last_arrived[0]
        for block in after(last_blocks, query_grad):
            last_sum = last_sum + block.astype(jnp.float32)
        pair_sum = pair_grad.astype(jnp.float32) + other_grad.astype(jnp.float32)
    else:
        last_arrived = sum_offsets(last_arrived)
        last_sum = last_arrived[0]
        for step in range(1, steps_back):
            arrived = lax.ppermute(last_arrived[step].astype(low), layer, line(dp_size, -step))
            last_sum = last_sum + arrived.astype(jnp.float32)
        query_grad, pair_grad = attend_back(qkv, pairs[0], plans[0], known, (), True, ())
        pair_grad = pair_grad.reshape(members, dp_size, 2 * HEAD_DIM, lanes)
        pair_grad = lax.all_to_all(pair_grad, layer, 0, 0, axis_index_groups=sharing, tiled=True)
        pair_sum = jnp.sum(pair_grad.astype(jnp.float32), axis=0)
    last_pair_grad = last_sum.astype(low)
    qkv_grad = jnp.concatenate((query_grad, pair_sum.astype(low)), axis=1)
    qkv_grad = lax.all_to_all(qkv_grad, layer, split_axis=0, concat_axis=0, tiled=True)
    qkv_grad = qkv_grad.reshape(slots, members, 3 * HEAD_DIM, lanes)
    last_qkv_grad = jnp.concatenate((last_query_grad[0], last_pair_grad), axis=0)

    units = jnp.stack((grad_up, grad_down)).reshape(2, 2 * column, tensor_size, half)
    units = units.transpose(2, 0, 1, 3)
    units = scatter_ring(units)
    zero = nothing(units)
    grad_normed_one = []
    for piece in range(members):
        product = jnp.einsum(
            "cfd,cft->dt", qkv_w, qkv_grad[:, piece], preferred_element_type=jnp.float32
        )
        product = (product + zero).astype(low).T.reshape(tensor_size, part, width)
        grad_normed_one.append(scatter_tensor(product))
    grad_normed_one = jnp.concatenate(grad_normed_one, axis=0)
    last_normed_one = lax.dot_general(
        last_qkv_grad, last_qkv_w, contract_first, preferred_element_type=jnp.float32
    )
    head = tensor_index * slots + lax.div(dp_index, members)
    own_sums = (jnp.sum(query_grad.astype(jnp.float32), axis=(0, 2)),)
    own_sums += (jnp.sum(pair_sum[:, HEAD_DIM:], axis=(0, 2)),)
    last_sums = jnp.sum(last_qkv_grad.astype(jnp.float32), axis=1).reshape(3, HEAD_DIM)
    qv_sum = jnp.zeros((2, HEADS, HEAD_DIM), jnp.float32).at[:, HEADS - 1].set(last_sums[::2])
    qv_sum = lax.dynamic_update_slice_in_dim(qv_sum, jnp.stack(own_sums)[:, None], head, 1)
    up_full = lax.dynamic_update_slice_in_dim(
        jnp.zeros((tensor_size, unit_slab), jnp.float32),
        grad_up_part.reshape(tensor_size, half),
        core_index * half,
        1,
    ).reshape(-1)
    early = jnp.concatenate(
        (grad_out_bias, grad_gain_two, grad_shift_two, grad_down_bias, up_full, qv_sum.reshape(-1))
    )
    early = butterfly(early)
    qv_sum = early[-2 * width :].reshape(2, width)
    early, up_sum = early[: 4 * width].reshape(4, width), early[4 * width : -2 * width]
    grad_normed_one = grad_normed_one + last_normed_one + nothing(early)
    grad_res_one, grad_gain_one, grad_shift_one = norm_backward(
        grad_normed_one, normed_one, inv_one, gain_one
    )
    grad_input = grad_stream_one + grad_res_one

    units = units.astype(low).reshape(2, 2, column, half)
    kept = pick(units, core_index, 1)
    arrived = other_core(pick(units, 1 - core_index, 1))
    units = (
        jnp.where(core_index == 0, kept, arrived),
        jnp.where(core_index == 0, arrived, kept),
    )
    units = jnp.concatenate(units, axis=2).astype(jnp.float32)
    grad_out = grad_out.reshape(2 * column, tensor_size, slab).transpose(1, 0, 2)
    grad_out = scatter_ring(grad_out).reshape(2, column, slab)
    sent = other_core(pick(grad_out, 1 - core_index, 0).astype(low))
    grad_out = (pick(grad_out, core_index, 0) + sent.astype(jnp.float32)).T

    own_qkv_grad = jnp.einsum(
        "gtd,cgft->dcf", wide_one, qkv_grad, preferred_element_type=jnp.float32
    )
    last_part = lax.dot_general(
        pre_one, last_qkv_grad, (((0,), (1,)), ((), ())), preferred_element_type=jnp.float32
    )
    grad_qkv = jnp.concatenate((own_qkv_grad.reshape(width, -1), last_part), axis=1).astype(low)
    if chips == 4:
        grad_qkv = grad_qkv.reshape(2, 2, 2, column, -1)
        sent = other_core(pick(grad_qkv, 1 - core_index, 2))
        kept = pick(grad_qkv, core_index, 2).astype(jnp.float32)
        grad_qkv = (kept + sent.astype(jnp.float32)).astype(low)
        grad_qkv = halve(grad_qkv, 1, flip(1), low_bit, None)
        grad_qkv = halve(grad_qkv, 0, flip(2), high_bit, None)
    else:
        grad_qkv = lax.psum_scatter(grad_qkv, layer, scatter_dimension=0, tiled=True)
    own_qkv_grad = grad_qkv[:, : 3 * head_rows].T.reshape(slots, 3, HEAD_DIM, column)
    own_qkv_grad = own_qkv_grad.transpose(1, 0, 2, 3).reshape(3, head_rows, column)
    last_part = grad_qkv[:, 3 * head_rows :].T.reshape(3, HEAD_DIM, column)
    last_sum = last_part.astype(jnp.float32)
    for source in range(tensor_size - 1):
        arrived = lax.ppermute(last_part, "tensor", [(source, tensor_size - 1)])
        last_sum = last_sum + arrived.astype(jnp.float32)
    grad_qkv = slab_rows(own_qkv_grad, last_sum.astype(low), slab, tensor_size, tensor_index)
    grad_qkv = grad_qkv.astype(jnp.float32)

    late = small_sum(jnp.stack((grad_gain_one, grad_shift_one)))
    grad_up_bias = lax.dynamic_slice_in_dim(up_sum, tensor_index * unit_slab, unit_slab, 0)
    return (
        block_out,
        grad_input,
        late[0],
        late[1],
        grad_qkv,
        qv_sum,
        grad_out,
        early[0],
        early[1],
        early[2],
        units[0],
        grad_up_bias,
        units[1].T,
        early[3],
    )


def solution(mesh):
    chips, tensor = mesh.shape["dp"] // 2, mesh.shape["tensor"]
    cores = jax.sharding.Mesh(mesh.devices.reshape(chips, 2, tensor), everywhere)
    in_specs = (
        P(everywhere, None),
        P(),
        P(),
        P(None, "tensor", None),
        P(),
        P("tensor", None),
        P(),
        P(),
        P(),
        P(None, "tensor"),
        P("tensor"),
        P("tensor", None),
        P(),
        P(),
        P(everywhere, None),
    )
    out_specs = (
        P(everywhere, None),
        P(everywhere, None),
        P(),
        P(),
        P(None, "tensor", layer),
        P(),
        P("tensor", layer),
        P(),
        P(),
        P(),
        P(layer, "tensor"),
        P("tensor"),
        P("tensor", layer),
        P(),
    )
    return jax.shard_map(local, mesh=cores, in_specs=in_specs, out_specs=out_specs, check_vma=False)
```
